32 devices in a mesh: grp: 2 (over core), tok: 16 (over z, y, x).
Axes of the slice: x: 2, y: 2, z: 4, core: 2. Of those that a mesh axis runs over, the one named last changes fastest.
Arguments:
- tokens: bfloat16 [32768, 1024], P(('grp', 'tok')), may hold values from -6 to 6
- enc_states: bfloat16 [32768, 1024], P(('grp', 'tok')), may hold values from -6 to 6
- dec_lengths: int32 [32, 4], P(('grp', 'tok')), may hold values from 1 to 512, 1024 in all within a row
- enc_lengths: int32 [32, 4], P(('grp', 'tok')), may hold values from 1 to 512, 1024 in all within a row
- cotangent: bfloat16 [32768, 1024], P(('grp', 'tok')), may hold values from -6 to 6
- self_query: bfloat16 [1024, 1024], P('tok'), may hold values from -0.1875 to 0.1875
- self_query_bias: bfloat16 [1024], P('tok'), may hold values from -3 to 3
- self_key: bfloat16 [1024, 1024], P('tok'), may hold values from -0.1875 to 0.1875
- self_value: bfloat16 [1024, 1024], P('tok'), may hold values from -0.1875 to 0.1875
- self_value_bias: bfloat16 [1024], P('tok'), may hold values from -3 to 3
- self_out: bfloat16 [1024, 1024], P('tok'), may hold values from -1.5 to 1.5
- self_out_bias: bfloat16 [1024], P('tok'), may hold values from -3 to 3
- first_gain: bfloat16 [1024], P('tok'), may hold values from 0.5 to 1.5
- first_shift: bfloat16 [1024], P('tok'), may hold values from -2 to 2
- cross_query: bfloat16 [1024, 1024], P('tok'), may hold values from -0.1875 to 0.1875
- cross_query_bias: bfloat16 [1024], P('tok'), may hold values from -3 to 3
- cross_key: bfloat16 [1024, 1024], P('tok'), may hold values from -0.1875 to 0.1875
- cross_value: bfloat16 [1024, 1024], P('tok'), may hold values from -0.1875 to 0.1875
- cross_value_bias: bfloat16 [1024], P('tok'), may hold values from -3 to 3
- cross_out: bfloat16 [1024, 1024], P('tok'), may hold values from -1.5 to 1.5
- cross_out_bias: bfloat16 [1024], P('tok'), may hold values from -3 to 3
- second_gain: bfloat16 [1024], P('tok'), may hold values from 0.5 to 1.5
- second_shift: bfloat16 [1024], P('tok'), may hold values from -2 to 2
- hidden_in: bfloat16 [1024, 4096], P('tok'), may hold values from -0.1875 to 0.1875
- hidden_in_bias: bfloat16 [4096], P('tok'), may hold values from -3 to 3
- hidden_out: bfloat16 [4096, 1024], P('tok'), may hold values from -0.09375 to 0.09375
- hidden_out_bias: bfloat16 [1024], P('tok'), may hold values from -2 to 2
- third_gain: bfloat16 [1024], P('tok'), may hold values from 0.5 to 1.5
- third_shift: bfloat16 [1024], P('tok'), may hold values from -2 to 2
- adapter_down: bfloat16 [512, 1024], P('tok'), may hold values from -0.1875 to 0.1875
- adapter_down_bias: bfloat16 [512], P('tok'), may hold values from -3 to 3
- adapter_up: bfloat16 [512, 1024], P('tok'), may hold values from -0.125 to 0.125
- adapter_up_bias: bfloat16 [1024], P('tok'), may hold values from -1 to 1
Outputs:
- layer_out: bfloat16 [32768, 1024], P(('grp', 'tok'))
- grad_tokens: bfloat16 [32768, 1024], P(('grp', 'tok'))
- grad_enc: bfloat16 [32768, 1024], P(('grp', 'tok'))
- grad_down: float32 [512, 1024], P('tok')
- grad_down_bias: float32 [512], P('tok')
- grad_up: float32 [512, 1024], P('tok')
- grad_up_bias: float32 [1024], P('tok')
The draws below stay inside these ranges and needn't reach their ends.
Inputs may be any that keep to these rules, and one draw needn't show every extreme that they name: `dec_lengths`: each row's 4 entries are the lengths of its runs of slots in order and sum to 1024; the last run is padding. `enc_lengths`: each row's 4 entries are the lengths of its runs of encoder slots in order and sum to 1024; run k of the encoder row belongs to run k of the decoder row.
All inputs are finite; a program needn't handle non-finite values.
Results may differ from the reference program's by a relative error of at most 0.023.
Values may be sent and summed in bfloat16 or wider, within the bound.
A program may use at most 448 MiB of HBM per device.

```python
import math
import jax
import jax.numpy as jnp
import numpy as np
from jax import lax

D = 1024
HEADS = 16
HEAD = 64
FF = 4096
BOT = 512
DOCS = 4
SLOTS = 1024
ENC = 1024
ROWS = 32
TOKENS = 32768
ENC_TOKENS = 32768


def raised(values, stream_key, source, target, blocks, factor):
    def block_of(position):
        return (jnp.arange(values.shape[position]) // (values.shape[position] // blocks)).reshape((-1,) + (1,) * (values.ndim - 1 - position))

    first = jax.random.permutation(stream_key, blocks)[block_of(target)]
    other_side = (block_of(target) + blocks // 2) % blocks
    return jnp.where((block_of(source) == first) | (block_of(source) == other_side), factor * values, values)


def block_levels(rng, shape, shards, smallest, top_value):
    gain = 1.0
    for axis_at, shards_of in shards:
        heights = jax.random.uniform(jax.random.fold_in(jax.random.fold_in(rng, 6), axis_at), (shards_of,), jnp.float32, smallest / len(shards), top_value / len(shards))
        gain = gain * jnp.repeat(jnp.exp(heights), shape[axis_at] // shards_of).reshape((-1,) + (1,) * (len(shape) - 1 - axis_at))
    return gain


def split_up(number_of, total, reach, lean):
    loads = [(1 << 20) // math.isqrt(standing ** lean) + 1 for standing in range(2, number_of + 1)]
    spare, given = total - reach - (number_of - 1), [1] * (number_of - 1)
    while spare > 0:
        candidates = [i for i in range(number_of - 1) if given[i] < reach]
        pool, remaining = sum([loads[i] for i in candidates]), spare
        for i in candidates:
            more = min(reach - given[i], max(1, remaining * loads[i] // pool), spare)
            given[i] = given[i] + more
            spare = spare - more
    return np.array([reach] + given)


def ragged(rng, count, total, reach, lean):
    if count == 2:
        one = jax.random.randint(rng, (), max(1, total - reach), min(reach, total - 1) + 1)
        return jnp.stack([one, total - one])
    sizes = jnp.asarray(split_up(count, total, reach, lean), jnp.int32)
    couples = (count - 1) // 2
    donor, receiver = sizes[1:1 + 2 * couples:2], sizes[2:2 + 2 * couples:2]
    margin = jnp.minimum(donor - 1, reach - receiver)
    shifted = jax.random.randint(jax.random.fold_in(rng, 1), (couples,), 0, 1 << 20) % (margin + 1)
    sizes = sizes.at[1:1 + 2 * couples:2].set(donor - shifted).at[2:2 + 2 * couples:2].set(receiver + shifted)
    return sizes[jax.random.permutation(jax.random.fold_in(rng, 2), count)]


def bell_draw(rng, extent, spread, bound, shards=(), kind=jnp.bfloat16):
    values = spread * jax.random.normal(rng, extent, jnp.float32)
    if shards:
        values = values * block_levels(rng, extent, shards, -0.22, 0.18)
    return jnp.clip(values, -bound, bound).astype(kind)


def noise_with(stream_key, shape, deviation, bound, split, heavy, held_as=jnp.bfloat16):
    values = deviation * jax.random.normal(stream_key, shape, jnp.float32)
    if split:
        values = values * block_levels(stream_key, shape, split, -0.22, 0.18)
    return jnp.clip(raised(values, jax.random.fold_in(stream_key, 3), *heavy), -bound, bound).astype(held_as)


def setup_inputs(seed: int = 0) -> dict:
    key_list = jax.random.split(jax.random.key(seed), 34)
    tokens = bell_draw(key_list[0], (TOKENS, D), 1.0, 6.0, ((0, 32),))
    enc_states = bell_draw(key_list[1], (ENC_TOKENS, D), 1.0, 6.0, ((0, 32),))
    dec_lengths = jax.vmap(lambda own: ragged(own, DOCS, SLOTS, SLOTS // 2, 2))(jax.random.split(key_list[2], ROWS)).reshape((ROWS, DOCS)).astype(jnp.int32)
    enc_lengths = jax.vmap(lambda own: ragged(own, DOCS, ENC, ENC // 2, 2))(jax.random.split(key_list[3], ROWS)).reshape((ROWS, DOCS)).astype(jnp.int32)
    cotangent = noise_with(key_list[4], (TOKENS, D), 1.0, 6.0, ((0, 32),), (0, 1, 32, 2.75))
    self_query = bell_draw(key_list[5], (D, D), D ** -0.5, 0.1875, ((0, 16),))
    self_query_bias = bell_draw(key_list[6], (D,), 0.5, 3.0, ((0, 16),))
    self_key = bell_draw(key_list[7], (D, D), D ** -0.5, 0.1875, ((0, 16),))
    self_value = bell_draw(key_list[8], (D, D), D ** -0.5, 0.1875, ((0, 16),))
    self_value_bias = bell_draw(key_list[9], (D,), 0.5, 3.0, ((0, 16),))
    self_out = bell_draw(key_list[10], (D, D), (D // 64) ** -0.5, 1.5, ((0, 16),))
    self_out_bias = bell_draw(key_list[11], (D,), 0.5, 3.0, ((0, 16),))
    first_gain = jnp.clip(1.0 + 0.1 * jax.random.normal(key_list[12], (D,), jnp.float32), 0.5, 1.5).astype(jnp.bfloat16)
    first_shift = bell_draw(key_list[13], (D,), 0.3, 2.0, ((0, 16),))
    cross_query = bell_draw(key_list[14], (D, D), D ** -0.5, 0.1875, ((0, 16),))
    cross_query_bias = bell_draw(key_list[15], (D,), 0.5, 3.0, ((0, 16),))
    cross_key = bell_draw(key_list[16], (D, D), D ** -0.5, 0.1875, ((0, 16),))
    cross_value = bell_draw(key_list[17], (D, D), D ** -0.5, 0.1875, ((0, 16),))
    cross_value_bias = bell_draw(key_list[18], (D,), 0.5, 3.0, ((0, 16),))
    cross_out = bell_draw(key_list[19], (D, D), (D // 64) ** -0.5, 1.5, ((0, 16),))
    cross_out_bias = bell_draw(key_list[20], (D,), 0.5, 3.0, ((0, 16),))
    second_gain = jnp.clip(1.0 + 0.1 * jax.random.normal(key_list[21], (D,), jnp.float32), 0.5, 1.5).astype(jnp.bfloat16)
    second_shift = bell_draw(key_list[22], (D,), 0.3, 2.0, ((0, 16),))
    hidden_in = bell_draw(key_list[23], (D, FF), D ** -0.5, 0.1875, ((0, 16),))
    hidden_in_bias = bell_draw(key_list[24], (FF,), 0.5, 3.0, ((0, 16),))
    hidden_out = bell_draw(key_list[25], (FF, D), FF ** -0.5, 0.09375, ((0, 16),))
    hidden_out_bias = bell_draw(key_list[26], (D,), 0.3, 2.0, ((0, 16),))
    third_gain = jnp.clip(1.0 + 0.1 * jax.random.normal(key_list[27], (D,), jnp.float32), 0.5, 1.5).astype(jnp.bfloat16)
    third_shift = bell_draw(key_list[28], (D,), 0.3, 2.0, ((0, 16),))
    adapter_down = bell_draw(key_list[29], (BOT, D), D ** -0.5, 0.1875, ((0, 16),))
    adapter_down_bias = bell_draw(key_list[30], (BOT,), 0.5, 3.0, ((0, 16),))
    adapter_up = bell_draw(key_list[31], (BOT, D), (4 * BOT) ** -0.5, 0.125, ((0, 16),))
    adapter_up_bias = bell_draw(key_list[32], (D,), 0.1, 1.0, ((0, 16),))
    return dict(tokens=tokens, enc_states=enc_states, dec_lengths=dec_lengths, enc_lengths=enc_lengths, cotangent=cotangent, self_query=self_query, self_query_bias=self_query_bias, self_key=self_key, self_value=self_value, self_value_bias=self_value_bias, self_out=self_out, self_out_bias=self_out_bias, first_gain=first_gain, first_shift=first_shift, cross_query=cross_query, cross_query_bias=cross_query_bias, cross_key=cross_key, cross_value=cross_value, cross_value_bias=cross_value_bias, cross_out=cross_out, cross_out_bias=cross_out_bias, second_gain=second_gain, second_shift=second_shift, hidden_in=hidden_in, hidden_in_bias=hidden_in_bias, hidden_out=hidden_out, hidden_out_bias=hidden_out_bias, third_gain=third_gain, third_shift=third_shift, adapter_down=adapter_down, adapter_down_bias=adapter_down_bias, adapter_up=adapter_up, adapter_up_bias=adapter_up_bias)


@jax.custom_vjp
def low(v):
    return lax.optimization_barrier(v.astype(jnp.bfloat16)).astype(jnp.float32)

@jax.custom_vjp
def low_back(v):
    return v

def low_keep(v):
    return (low(v), None)

def low_pass(kept, grad):
    return (grad,)

def back_keep(v):
    return (v, None)

def back_low(kept, grad):
    return (low(grad),)
low.defvjp(low_keep, low_pass)
low_back.defvjp(back_keep, back_low)
highest = lax.Precision.HIGHEST
epsilon = 1e-05
adapter_scale = 4.0

def matmul(left, right):
    return jnp.dot(left, right, precision=highest, preferred_element_type=jnp.float32)

def both_round(values):
    return low_back(low(values))

def layer_norm(inputs, norm_gain, norm_shift):
    average = lax.optimization_barrier(jnp.mean(inputs, axis=-1, keepdims=True))
    centred = inputs - average
    variance = lax.optimization_barrier(jnp.mean(centred * centred, axis=-1, keepdims=True))
    return centred * lax.rsqrt(variance + epsilon) * norm_gain + norm_shift

def segment_ids(lengths, total_slots):
    ends = jnp.cumsum(lengths).astype(jnp.int32)
    positions = jnp.arange(total_slots, dtype=jnp.int32)
    return lax.optimization_barrier(jnp.sum((positions[:, None] >= ends[None, :]).astype(jnp.int32), axis=1)).astype(jnp.int32)

def attention(query_in, key_in, frozen, prefix, allowed):
    queries = both_round(matmul(query_in, frozen[prefix + '_query']) + frozen[prefix + '_query_bias'])
    key_rows = both_round(matmul(key_in, frozen[prefix + '_key']))
    value_rows = both_round(matmul(key_in, frozen[prefix + '_value']) + frozen[prefix + '_value_bias'])
    query_count = queries.shape[0]
    key_count = key_rows.shape[0]
    heads_q = queries.reshape(query_count, HEADS, HEAD)
    heads_k = key_rows.reshape(key_count, HEADS, HEAD)
    heads_v = value_rows.reshape(key_count, HEADS, HEAD)
    scores = low_back(jnp.einsum('qhd,khd->hqk', heads_q, heads_k, precision=highest) * HEAD ** (-0.5))
    scores = jnp.where(allowed[None], scores, -1000000000.0)
    attn_probs = low(jax.nn.softmax(scores, axis=-1))
    mixed = jnp.einsum('hqk,khd->qhd', attn_probs, heads_v, precision=highest).reshape(query_count, D)
    mixed = both_round(mixed)
    return low_back(matmul(mixed, frozen[prefix + '_out']) + frozen[prefix + '_out_bias'])

def row_forward(frozen, dec_seg, enc_seg, inputs, encoded, down_w, down_b, up_w, up_b):
    positions = jnp.arange(SLOTS, dtype=jnp.int32)
    self_allowed = (dec_seg[:, None] == dec_seg[None, :]) & (positions[None, :] <= positions[:, None])
    cross_allowed = dec_seg[:, None] == enc_seg[None, :]
    first_sum = inputs + attention(inputs, inputs, frozen, 'self', self_allowed)
    first_norm = layer_norm(first_sum, frozen['first_gain'], frozen['first_shift'])
    second_sum = first_norm + attention(low(first_norm), encoded, frozen, 'cross', cross_allowed)
    second_norm = layer_norm(second_sum, frozen['second_gain'], frozen['second_shift'])
    second_low = low(second_norm)
    hidden_pre = low_back(matmul(second_low, frozen['hidden_in']) + frozen['hidden_in_bias'])
    hidden_act = low(jax.nn.gelu(hidden_pre, approximate=False))
    ffn_out = low_back(matmul(hidden_act, frozen['hidden_out']) + frozen['hidden_out_bias'])
    bottle_pre = low_back(matmul(second_low, down_w.T) + down_b)
    bottle_act = low(jax.nn.gelu(bottle_pre, approximate=False))
    adapter_out = low_back(matmul(bottle_act, up_w) + up_b)
    third_sum = second_norm + ffn_out + adapter_scale * adapter_out
    return layer_norm(third_sum, frozen['third_gain'], frozen['third_shift'])
frozen_names = ('self_query', 'self_query_bias', 'self_key', 'self_value', 'self_value_bias', 'self_out', 'self_out_bias', 'first_gain', 'first_shift', 'cross_query', 'cross_query_bias', 'cross_key', 'cross_value', 'cross_value_bias', 'cross_out', 'cross_out_bias', 'second_gain', 'second_shift', 'hidden_in', 'hidden_in_bias', 'hidden_out', 'hidden_out_bias', 'third_gain', 'third_shift')

def reference(tokens, enc_states, dec_lengths, enc_lengths, cotangent, self_query, self_query_bias, self_key, self_value, self_value_bias, self_out, self_out_bias, first_gain, first_shift, cross_query, cross_query_bias, cross_key, cross_value, cross_value_bias, cross_out, cross_out_bias, second_gain, second_shift, hidden_in, hidden_in_bias, hidden_out, hidden_out_bias, third_gain, third_shift, adapter_down, adapter_down_bias, adapter_up, adapter_up_bias):
    frozen_arrays = (self_query, self_query_bias, self_key, self_value, self_value_bias, self_out, self_out_bias, first_gain, first_shift, cross_query, cross_query_bias, cross_key, cross_value, cross_value_bias, cross_out, cross_out_bias, second_gain, second_shift, hidden_in, hidden_in_bias, hidden_out, hidden_out_bias, third_gain, third_shift)
    frozen = {name: array.astype(jnp.float32) for name, array in zip(frozen_names, frozen_arrays)}
    adapter_params = (adapter_down.astype(jnp.float32), adapter_down_bias.astype(jnp.float32), adapter_up.astype(jnp.float32), adapter_up_bias.astype(jnp.float32))
    input_rows = tokens.astype(jnp.float32).reshape(ROWS, SLOTS, D)
    encoded_rows = enc_states.astype(jnp.float32).reshape(ROWS, ENC, D)
    upstream_rows = cotangent.astype(jnp.float32).reshape(ROWS, SLOTS, D)

    def one_row(totals, items):
        row_in, row_enc, row_up, row_dec, row_enc_len = items
        dec_seg = segment_ids(row_dec, SLOTS)
        enc_seg = segment_ids(row_enc_len, ENC)
        valid = (dec_seg < DOCS - 1).astype(jnp.float32)

        def forward(inputs, encoded, down_w, down_b, up_w, up_b):
            return row_forward(frozen, dec_seg, enc_seg, inputs, encoded, down_w, down_b, up_w, up_b)
        output, pullback = jax.vjp(forward, row_in, row_enc, *adapter_params)
        grads = pullback(row_up * valid[:, None])
        totals = jax.tree.map(jnp.add, totals, tuple(grads[2:]))
        return (totals, (output.astype(jnp.bfloat16), grads[0].astype(jnp.bfloat16), grads[1].astype(jnp.bfloat16)))
    zeros = tuple((jnp.zeros_like(param) for param in adapter_params))
    totals, (outputs, grad_in, grad_encoded) = lax.scan(one_row, zeros, (input_rows, encoded_rows, upstream_rows, dec_lengths, enc_lengths))
    return (outputs.reshape(TOKENS, D), grad_in.reshape(TOKENS, D), grad_encoded.reshape(ENC_TOKENS, D), totals[0], totals[1], totals[2], totals[3])
```

```python
import functools

import jax
import jax.numpy as jnp
from jax import lax
from jax.experimental import pallas as pl
from jax.experimental.pallas import tpu as pltpu
from jax.sharding import PartitionSpec as P

F32 = jnp.float32
BF16 = jnp.bfloat16
HEAD = 64
PAIR = 2 * HEAD
EPSILON = 1e-05
SCALE = 4.0
RB = 256
QB = 128
FAR = float(1 << 30)
MIB = 1 << 20
VMEM = 62 * MIB
MESH = pl.DeviceIdType.MESH
ANY = pl.BlockSpec(memory_space=pl.ANY)
SMEM = pl.BlockSpec(memory_space=pltpu.SMEM)
WHOLE = pl.BlockSpec(memory_space=pltpu.VMEM)


def dot(a, b):
    return jnp.dot(a, b, preferred_element_type=F32)


def dot_nt(a, b):
    return lax.dot_general(a, b, (((1,), (1,)), ((), ())), preferred_element_type=F32)


def dot_tn(a, b):
    return lax.dot_general(a, b, (((0,), (0,)), ((), ())), preferred_element_type=F32)


def cost(macs, *arrays):
    return pl.CostEstimate(flops=2 * macs, bytes_accessed=sum(a.size * a.dtype.itemsize for a in arrays), transcendentals=0)


def rows_of(i):
    return pl.ds(pl.multiple_of(i * RB, RB), RB)


def lanes_of(p):
    return pl.ds(pl.multiple_of(p * PAIR, PAIR), PAIR)


def two_heads(values):
    row = lax.broadcasted_iota(jnp.int32, values.shape, 0)
    zero = jnp.zeros_like(values)
    return jnp.concatenate([jnp.where(row < HEAD, values, zero), jnp.where(row < HEAD, zero, values)], axis=1)


def one_of_each(values):
    n = values.shape[1] // 2
    row = lax.broadcasted_iota(jnp.int32, (values.shape[0], n), 0)
    return jnp.where(row < HEAD, values[:, :n], values[:, n:])


def twice(values):
    return jnp.concatenate([values, values], axis=1)


def normalized(r):
    centred = r - jnp.mean(r, axis=-1, keepdims=True)
    rstd = lax.rsqrt(jnp.mean(centred * centred, axis=-1, keepdims=True) + EPSILON)
    return centred * rstd, rstd


def norm_back(xhat, rstd, gain, upstream):
    u = upstream * gain
    first = jnp.mean(u, axis=-1, keepdims=True)
    second = jnp.mean(u * xhat, axis=-1, keepdims=True)
    return (u - first - xhat * second) * rstd


def gelu_parts(v):
    size = jnp.abs(v)
    bell = jnp.exp(-0.5 * v * v)
    t = 1.0 / (1.0 + 0.23164188 * size)
    poly = t * (0.127414796 + t * (-0.142248368 + t * (0.71070687 + t * (-0.726576013 + t * 0.530702714))))
    tail = poly * bell
    phi = jnp.where(v < 0, tail, 1.0 - tail)
    return v * phi, phi + (0.3989422804014327 * v) * bell


def ends_of(ref):
    e0 = ref[0, 0]
    e1 = e0 + ref[0, 1]
    return e0, e1, e1 + ref[0, 2]


def segment(position, ends):
    return sum((position >= e).astype(jnp.int32) for e in ends)


def key_features(ref, ends):
    def block(i, _):
        shape = (RB, ref.shape[1])
        seg = segment(lax.broadcasted_iota(jnp.int32, shape, 0) + i * RB, ends)
        lane = lax.broadcasted_iota(jnp.int32, shape, 1)
        ref[rows_of(i), :] = ((lane == seg) | ((lane >= 4) & (lane < 7))).astype(F32).astype(BF16)
        return 0

    lax.fori_loop(0, ref.shape[0] // RB, block, 0)


def query_features(first, count, ends):
    seg = segment(lax.broadcasted_iota(jnp.int32, (16, count), 1) + first, ends)
    row = lax.broadcasted_iota(jnp.int32, (16, count), 0)
    return jnp.where((row < 4) & (row != seg), -FAR, 0.0)


def in_parts(values, row):
    at = lax.broadcasted_iota(jnp.int32, (16, values.shape[1]), 0)
    high = values.astype(BF16).astype(F32)
    middle = (values - high).astype(BF16).astype(F32)
    low = values - high - middle
    return jnp.where(at == row, high, jnp.where(at == row + 1, middle, jnp.where(at == row + 2, low, 0.0)))


def pick(seg, ends, first, last):
    e0, e1, e2 = ends
    start = jnp.where(seg == 0, first, jnp.where(seg == 1, e0, jnp.where(seg == 2, e1, e2)))
    stop = jnp.where(seg == 0, e0, jnp.where(seg == 1, e1, jnp.where(seg == 2, e2, last)))
    return start, stop


NZ, NB = 4, 4


def pieces(shapes):
    found = []
    for a, (rows, cols) in enumerate(shapes):
        if rows >= 256:
            found += [(a, j, 4, 0, 1, j > 1) for j in range(4)]
        elif cols >= 4096:
            found += [(a, 0, 1, j, 8, True) for j in range(8)]
        else:
            found.append((a, 0, 1, 0, 1, False))
    return found


class Gather:
    RATE = 0.086

    def __init__(self, ins, outs, stages, sems):
        self.ins, self.outs, self.stages = ins, outs, stages
        self.in_s, self.own_s, self.zs, self.zr, self.ws, self.wr, self.ps, self.pr = sems
        self.core, t = lax.axis_index("grp"), lax.axis_index("tok")
        self.z, b = t // NB, t % NB
        y, x = b // 2, b % 2
        by_x, by_y = y * 2 + (1 - x), (1 - y) * 2 + x
        self.b = b
        self.n2 = by_x + self.core * (by_y - by_x)
        self.n3 = by_y + self.core * (by_x - by_y)
        self.pieces = pieces([r.shape for r in ins])
        count = len(self.pieces)
        self.size = []
        for a, _, rn, _, cn, _ in self.pieces:
            rows, cols = ins[a].shape
            self.size.append(NZ * NB * rows * cols * 2 / (rn * cn) / MIB)
        self.now, self.short, self.swaps, self.long = 5.0, 5.0, 0.0, 8.0
        self.next = [0] * 5
        self.detour = [i for i in range(count) if self.pieces[i][5]]
        self.arrive = {}

    def dev(self, core, z, b):
        return {"grp": core, "tok": z * NB + b}

    def peers(self):
        c, z, b = self.core, self.z, self.b
        along = [self.dev(c, (z + d) % NZ, b) for d in (1, 2, 3)]
        return along + [self.dev(c, z, self.n2), self.dev(c, z, self.n3), self.dev(1 - c, z, b)]

    def barrier(self):
        sem = pltpu.get_barrier_semaphore()
        peers = self.peers()
        for p in peers:
            pl.semaphore_signal(sem, inc=1, device_id=p, device_id_type=MESH)
        pl.semaphore_wait(sem, len(peers))

    def cut(self, i):
        a, rj, rn, cj, cn, _ = self.pieces[i]
        rows, cols = self.ins[a].shape
        r, c = rows // (2 * rn), cols // cn
        first = pl.multiple_of(self.core * (rows // 2) + rj * r, r)
        return a, pl.ds(first, r), pl.ds(rj * r, r), pl.ds(cj * c, c)

    def half(self, a):
        rows = self.ins[a].shape[0] // 2
        return pl.ds(pl.multiple_of(self.core * rows, rows), rows)

    def staged(self, a):
        return pltpu.make_async_copy(self.ins[a].at[self.half(a)], self.stages[a], self.in_s.at[a])

    def own(self, a):
        return pltpu.make_async_copy(self.stages[a], self.outs[a].at[self.z, self.b, self.half(a)], self.own_s.at[a])

    def along_z(self, i, d):
        a, r, here, c = self.cut(i)
        return pltpu.make_async_remote_copy(
            self.stages[a].at[here, c], self.outs[a].at[self.z, self.b, r, c],
            self.zs.at[i, d - 1], self.zr.at[i, d - 1],
            device_id=self.dev(self.core, (self.z + d) % NZ, self.b), device_id_type=MESH,
        )

    def aside(self, i):
        a, r, here, c = self.cut(i)
        return pltpu.make_async_remote_copy(
            self.stages[a].at[here, c], self.outs[a].at[self.z, self.b, r, c], self.ps.at[i, 0], self.pr.at[i, 0],
            device_id=self.dev(self.core, self.z, self.n2), device_id_type=MESH,
        )

    def along_z_too(self, i, d):
        a, r, _, c = self.cut(i)
        ref = self.outs[a].at[self.z, self.n2, r, c]
        return pltpu.make_async_remote_copy(
            ref, ref, self.ws.at[i, d - 1], self.wr.at[i, d - 1],
            device_id=self.dev(self.core, (self.z + d) % NZ, self.b), device_id_type=MESH,
        )

    def column(self, i, b, k, to):
        a, r, _, c = self.cut(i)
        ref = self.outs[a].at[:, b, r, c]
        return pltpu.make_async_remote_copy(
            ref, ref, self.ps.at[i, k], self.pr.at[i, k],
            device_id=self.dev(self.core, self.z, to), device_id_type=MESH,
        )

    def second(self, i):
        return self.column(i, self.b, 0, self.n2)

    def third(self, i):
        return self.column(i, self.b, 1, self.n3)

    def onward(self, i):
        return self.column(i, self.n2, 2, self.n3)

    def swap(self, i):
        a, r, _, c = self.cut(i)
        ref = self.outs[a].at[:, :, r, c]
        return pltpu.make_async_remote_copy(
            ref, ref, self.ps.at[i, 3], self.pr.at[i, 3],
            device_id=self.dev(1 - self.core, self.z, self.b), device_id_type=MESH,
        )

    def begin(self):
        for a in range(len(self.ins)):
            self.staged(a).wait()
            self.own(a).start()
            for i, piece in enumerate(self.pieces):
                if piece[0] == a:
                    for d in (1, 2, 3):
                        self.along_z(i, d).start()
                    self.long += self.size[i] / 4 / self.RATE
                    self.arrive["z", i] = self.long
                    if piece[5]:
                        self.aside(i).start()
                        self.short += self.size[i] / 32 / self.RATE
                        self.arrive["aside", i] = self.short + 1

    def ready(self, kind):
        at = self.next[kind]
        if kind == 4:
            return self.arrive["aside", self.detour[at]] if at < len(self.detour) else None
        if at >= len(self.pieces):
            return None
        names = (("z",), ("z2",) if self.pieces[at][5] else ("second",), ("third", "onward"), ("swap",))[kind]
        when = [self.arrive.get((name, at)) for name in names]
        return None if None in when else max(when)

    def event(self, kind):
        self.now = max(self.now, self.ready(kind)) + 0.15
        at = self.next[kind]
        self.next[kind] += 1
        i = self.detour[at] if kind == 4 else at
        a, rj, _, cj, _, detour = self.pieces[i]
        link = self.size[i] / 8 / self.RATE

        def sent(name):
            self.short = max(self.short, self.now) + link
            self.arrive[name, i] = self.short + 1

        if kind == 0:
            if rj == 0 and cj == 0:
                self.own(a).wait()
            for d in (1, 2, 3):
                self.along_z(i, d).wait_recv()
            if not detour:
                self.second(i).start()
                sent("second")
            self.third(i).start()
            sent("third")
        elif kind == 1:
            if detour:
                for d in (1, 2, 3):
                    self.along_z_too(i, d).wait_recv()
            else:
                self.second(i).wait_recv()
            self.onward(i).start()
            sent("onward")
        elif kind == 2:
            self.third(i).wait_recv()
            self.onward(i).wait_recv()
            self.swap(i).start()
            self.swaps = max(self.swaps, self.now) + self.size[i] * 0.86
            self.arrive["swap", i] = self.swaps + 1.5
        elif kind == 3:
            self.swap(i).wait_recv()
        else:
            self.aside(i).wait_recv()
            for d in (1, 2, 3):
                self.along_z_too(i, d).start()
            self.long = max(self.long, self.now) + self.size[i] / 4 / self.RATE
            self.arrive["z2", i] = self.long

    def pump(self):
        going = True
        while going:
            going = False
            for kind in (4, 1, 2, 3, 0):
                when = self.ready(kind)
                if when is not None and when <= self.now and (kind or self.short - self.now < 7):
                    self.event(kind)
                    going = True
                    break

    def passed(self, us):
        self.now += us
        self.pump()

    def until(self, last):
        while self.next[3] <= last:
            self.pump()
            if self.next[3] <= last:
                late = [(self.ready(k) + (max(0, self.short - self.now - 7) if k == 0 else 0), -k) for k in range(5) if self.ready(k) is not None]
                self.event(-min(late)[1])

    def whole(self, a):
        self.until(max(i for i, p in enumerate(self.pieces) if p[0] == a))

    def part(self, a, j):
        self.until([i for i, p in enumerate(self.pieces) if p[0] == a][j])

    def finish(self):
        self.until(len(self.pieces) - 1)
        for i, piece in enumerate(self.pieces):
            for d in (1, 2, 3):
                self.along_z(i, d).wait_send()
                if piece[5]:
                    self.along_z_too(i, d).wait_send()
            for copy in (self.aside if piece[5] else self.second, self.third, self.onward, self.swap):
                copy(i).wait_send()


def gather_scratch(shapes):
    n, k = len(shapes), len(pieces(shapes))
    dma = pltpu.SemaphoreType.DMA
    return [pltpu.VMEM((r // 2, c), BF16) for r, c in shapes] + [dma((n,)), dma((n,)), dma((k, 3)), dma((k, 3)), dma((k, 3)), dma((k, 3)), dma((k, 4)), dma((k, 4))]


SQB, SVB, SOB, G1, S1, CQB, CVB, COB, G2, S2, HOB, G3, S3, AUB = ((p % 2) * 8 + p // 2 for p in range(14))


def pack_vectors(vectors, hidden_bias, down_bias, groups):
    total, at = 0, 0
    for v in (*vectors, hidden_bias, down_bias):
        part = v.reshape(groups, -1) if groups > 1 else v
        more = part.shape[-1]
        total = total + jnp.pad(part, [(0, 0)] * (part.ndim - 1) + [(at, 4096 - at - more)])
        at += more
    return total.reshape(groups, 32, 128)


def unpack_vectors(packed, vec, hidden_bias, down_bias):
    lane = lax.broadcasted_iota(jnp.int32, (16, 128), 1)
    blocks = [packed[t][:16].astype(F32) for t in range(16)]
    turned = [pltpu.roll(b, HEAD, 1) for b in blocks]
    for u in range(8):
        cols = slice(u * 128, (u + 1) * 128)
        vec[0:8, cols] = jnp.where(lane < HEAD, blocks[2 * u], turned[2 * u + 1])[:8]
        vec[8:16, cols] = jnp.where(lane < HEAD, turned[2 * u], blocks[2 * u + 1])[:8]
    for t in range(16):
        for j in range(2):
            first = t * 256 + j * 128
            hidden_bias[:, first : first + 128] = blocks[t][7 + j : 8 + j]
    for u in range(4):
        row = blocks[4 * u]
        for j in range(1, 4):
            row = jnp.where(lane < 32 * j, row, pltpu.roll(blocks[4 * u + j], 32 * j, 1))
        down_bias[:, u * 128 : (u + 1) * 128] = row[9:10]


WEIGHTS = 12
SQ, SK, SV, CK, CV, SO, CQ, CO, DOWN, UP, HOUT, HIN = range(WEIGHTS)
VEC = 0


def attend_block(i, extent, causal, q_t, k, v_t, k_feat, q_feat, mix, mix_t, lse, even, odd):
    cols = pl.ds(i * QB if isinstance(i, int) else pl.multiple_of(i * QB, QB), QB)
    chunks = [(a, min(RB, extent - a)) for a in range(0, extent, RB)]
    empty = jnp.zeros((PAIR - 16, 2 * QB), BF16)

    def step(p, before, now):
        if before is not None:
            peak = jnp.full((8, 2 * QB), -3e38, F32)
            for a, w in chunks:
                peak = jnp.maximum(peak, jnp.max(before[a : a + w, :].reshape(w // 8, 8, 2 * QB), axis=0))
            peak = jnp.max(peak, axis=0, keepdims=True)
            total = jnp.zeros((8, 2 * QB), F32)
            acc = jnp.zeros((PAIR, 2 * QB), F32)
        if now is not None:
            wide = jnp.concatenate([two_heads(q_t[lanes_of(p + 1), cols]), twice(q_feat[:, cols]), empty], axis=0)
        for a, w in chunks:
            if now is not None:
                s = dot(jnp.concatenate([k[a : a + w, lanes_of(p + 1)], k_feat[a : a + w, :]], axis=1), wide)
                if causal and a + w == extent:
                    key = lax.broadcasted_iota(jnp.int32, (w, 2 * QB), 0) + a
                    query = lax.broadcasted_iota(jnp.int32, (w, 2 * QB), 1) % QB + i * QB
                    s = jnp.where(key <= query, s, -FAR)
                now[a : a + w, :] = s
            if before is not None:
                e = jnp.exp(before[a : a + w, :] - peak)
                total = total + jnp.sum(e.reshape(w // 8, 8, 2 * QB), axis=0)
                acc = acc + dot(v_t[lanes_of(p), a : a + w], e.astype(BF16))
        if before is not None:
            total = jnp.sum(total, axis=0, keepdims=True)
            out = one_of_each(acc * (1.0 / total)).astype(BF16)
            mix_t[lanes_of(p), cols] = out
            mix[cols, lanes_of(p)] = jnp.transpose(out)
            both = peak + jnp.log(total)
            lse[p, 0:1, cols] = both[:, :QB]
            lse[p, 1:2, cols] = both[:, QB:]

    pairs = q_t.shape[0] // PAIR

    def loop(g, _):
        step(2 * g, even, odd)
        step(2 * g + 1, odd, even)
        return 0

    step(-1, None, even)
    lax.fori_loop(0, pairs // 2 - 1, loop, 0)
    step(pairs - 2, even, odd)
    step(pairs - 1, odd, None)


SAVED = 16
(O_SQ, O_SK, O_SV, O_SM, O_CQ, O_CK, O_CV, O_CM, O_XH1, O_XH2, O_X2B, O_DH, O_DB, O_AB, O_R3, O_STAT) = range(SAVED)


def forward_kernel(remote, *refs):
    tokens, enc, dec_len, enc_len = refs[:4]
    arrays, refs = refs[4 : 5 + WEIGHTS], refs[5 + WEIGHTS :]
    gather = None
    if remote:
        extra = len(arrays) + 8
        gather = Gather(arrays, refs[: 1 + WEIGHTS], refs[-extra:-8], refs[-8:])
        arrays, refs = refs[: 1 + WEIGHTS], refs[1 + WEIGHTS : -extra]

    saved = refs[:SAVED]
    lse1, lse2, vec = refs[SAVED : SAVED + 3]
    (pool, even, odd, kf1, kf2, qf, xf, wslots, oslots, aslots, dbot, abot, stat, packed, hb, db, pool_s, w_s, out_s) = refs[SAVED + 3 :]
    X, ENC, QS, KS, VS, KC, VC, MIX, MTS, X1B, XH1, QC, MTC, X2B, XH2 = range(15)
    VTS, VTC = XH1, XH2
    DG = (X, ENC, KC, VC)
    n_rows = pool.shape[1] // RB

    loads = [pltpu.make_async_copy(tokens, pool.at[X], pool_s.at[0]), pltpu.make_async_copy(enc, pool.at[ENC], pool_s.at[1])]
    if gather is not None:
        for a in range(len(arrays)):
            gather.staged(a).start()
    for c in loads:
        c.start()
    if gather is not None:
        gather.barrier()
        gather.begin()

    free_slots = wslots.shape[0]
    fetches, slot_of = {}, {}
    for k, w in enumerate((SQ, SK, SV, CK, CV, SO, CQ, CO)):
        fetches[w], slot_of[w] = (arrays[1 + w], wslots.at[k % free_slots]), (0, k % free_slots, None)
    for k, w in enumerate((DOWN, UP)):
        fetches[w], slot_of[w] = (arrays[1 + w], aslots.at[k]), (1, k, None)
    for j in range(4):
        for h in range(2):
            if h == 0:
                fetches[HOUT, j] = (arrays[1 + HOUT].at[j], oslots.at[j % oslots.shape[0]])
                slot_of[HOUT, j] = (2, j % oslots.shape[0], None)
            at = slice(h * 512, (h + 1) * 512)
            source = arrays[1 + HIN].at[:, :, :, j * 1024 + h * 512 : j * 1024 + (h + 1) * 512]
            fetches[HIN, 2 * j + h] = (source, wslots.at[j % free_slots, :, :, :, at])
            slot_of[HIN, 2 * j + h] = (0, j % free_slots, h)
    order = list(fetches)

    def copy_of(k):
        return pltpu.make_async_copy(*fetches[k], w_s.at[order.index(k)])

    started, used = [], set()

    def arrived(k):
        return gather is None or gather.next[3] > piece_of(k)

    def piece_of(k):
        a, j = (k, None) if isinstance(k, int) else k
        found = [i for i, p in enumerate(gather.pieces) if p[0] == 1 + a]
        return found[j] if a == HIN else found[-1]

    def ahead(k):
        kind, slot, half = slot_of[k]
        before = [u for u in order[: order.index(k)] if slot_of[u][:2] == (kind, slot)]
        return all(u in used for u in before if half is None or slot_of[u][2] in (None, half))

    def prefetch():
        while len(started) < len(order) and arrived(order[len(started)]) and ahead(order[len(started)]):
            copy_of(order[len(started)]).start()
            started.append(order[len(started)])

    def passed(us):
        if gather is not None:
            gather.passed(us)
        prefetch()

    def weight(k):
        if gather is not None:
            gather.until(piece_of(k))
        prefetch()
        assert k in started
        copy_of(k).wait()
        ref = fetches[k][1]
        return lambda: ref[...].reshape(-1, ref.shape[-1])

    writes = []

    def write(src, slot, dst=None):
        c = pltpu.make_async_copy(src, saved[slot] if dst is None else dst, out_s.at[len(writes)])
        c.start()
        writes.append(c)

    dec_ends, enc_ends = ends_of(dec_len), ends_of(enc_len)
    key_features(kf1, dec_ends)
    key_features(kf2, enc_ends)
    qf[...] = query_features(0, qf.shape[1], dec_ends).astype(BF16)
    if gather is not None:
        gather.whole(VEC)
    packed_in = pltpu.make_async_copy(arrays[VEC], packed, pool_s.at[2])
    packed_in.start()
    packed_in.wait()
    unpack_vectors([packed[t // NB, t % NB] for t in range(NZ * NB)], vec, hb, db)
    for c in loads:
        c.wait()

    def project(src, w, dst, b=None, factor=None, turned=None):
        get = weight(w)

        def block(i, _):
            r = dot(pool[src, rows_of(i), :], get())
            if b is not None:
                r = r + vec[b : b + 1, :]
            r = r.astype(BF16)
            if factor is not None:
                r = r * jnp.asarray(factor, BF16)
            if dst is not None:
                pool[dst, rows_of(i), :] = r
            if turned is not None:
                pool[turned, :, rows_of(i)] = jnp.transpose(r)
            return 0

        lax.fori_loop(0, n_rows, block, 0)
        used.add(w)
        passed(3)

    shrink = HEAD ** (-0.5)
    project(X, SQ, None, SQB, shrink, QS)
    project(X, SK, KS)
    project(X, SV, VS, SVB, None, VTS)
    write(pool.at[QS], O_SQ)
    write(pool.at[KS], O_SK)
    write(pool.at[VS], O_SV)
    n_blocks = pool.shape[1] // QB
    for i in range(n_blocks):
        attend_block(i, (i + 1) * QB, True, pool.at[QS], pool.at[KS], pool.at[VTS], kf1, qf, pool.at[MIX], pool.at[MTS], lse1, even, odd)
        passed(0.62 * (i + 1))
    write(pool.at[MTS], O_SM)
    project(ENC, CK, KC)
    project(ENC, CV, VC, CVB, None, VTC)
    write(pool.at[KC], O_CK)
    write(pool.at[VC], O_CV)

    def mix_out(mixed, w, b, residual, gain, shift, low_slot, hat_slot, column):
        get = weight(w)

        def block(i, _):
            r = residual(i) + dot(pool[mixed, rows_of(i), :], get()) + vec[b : b + 1, :]
            xhat, rstd = normalized(r)
            y = xhat * vec[gain : gain + 1, :] + vec[shift : shift + 1, :]
            xf[rows_of(i), :] = y
            pool[low_slot, rows_of(i), :] = y.astype(BF16)
            pool[hat_slot, rows_of(i), :] = xhat.astype(BF16)
            stat[column, rows_of(i), :] = jnp.broadcast_to(rstd, (RB, 128))
            return 0

        lax.fori_loop(0, n_rows, block, 0)
        used.add(w)
        passed(4)

    mix_out(MIX, SO, SOB, lambda i: pool[X, rows_of(i), :].astype(F32), G1, S1, X1B, XH1, 0)
    write(pool.at[XH1], O_XH1)
    project(X1B, CQ, None, CQB, shrink, QC)
    write(pool.at[QC], O_CQ)
    for part in range(4):

        def block(i, _):
            attend_block(i, pool.shape[1], False, pool.at[QC], pool.at[KC], pool.at[VTC], kf2, qf, pool.at[MIX], pool.at[MTC], lse2, even, odd)
            return 0

        lax.fori_loop(part * n_blocks // 4, (part + 1) * n_blocks // 4, block, 0)
        passed(8)
    write(pool.at[MTC], O_CM)
    mix_out(MIX, CO, COB, lambda i: xf[rows_of(i), :], G2, S2, X2B, XH2, 1)
    write(pool.at[XH2], O_XH2)
    write(pool.at[X2B], O_X2B)
    write(stat, O_STAT)

    down, up = weight(DOWN), weight(UP)

    def adapter(i, _):
        pre = dot_nt(pool[X2B, rows_of(i), :], down()) + db[...]
        act, slope = gelu_parts(pre)
        low = act.astype(BF16)
        abot[rows_of(i), :] = low
        dbot[rows_of(i), :] = slope.astype(BF16)
        more = dot(low, up()) + vec[AUB : AUB + 1, :]
        xf[rows_of(i), :] = xf[rows_of(i), :] + vec[HOB : HOB + 1, :] + SCALE * more
        return 0

    lax.fori_loop(0, n_rows, adapter, 0)
    passed(5)
    write(abot, O_AB)
    write(dbot, O_DB)
    for c in writes[:7]:
        c.wait()
    for j in range(8):
        if j % 2 == 0:
            w_out = weight((HOUT, j // 2))
        w_in = weight((HIN, j))
        at, rows_at = slice(j * 512, (j + 1) * 512), slice(j % 2 * 512, j % 2 * 512 + 512)

        def into(i, w_in=w_in, at=at):
            return dot(pool[X2B, rows_of(i), :], w_in()) + hb[:, at]

        def out_of(i, pre, j=j, w_out=w_out, rows_at=rows_at):
            act, slope = gelu_parts(pre)
            pool[DG[j // 2], rows_of(i), rows_at] = slope.astype(BF16)
            xf[rows_of(i), :] = xf[rows_of(i), :] + dot(act.astype(BF16), w_out()[rows_at, :])

        def hidden(g, _):
            first, second = into(2 * g), into(2 * g + 1)
            out_of(2 * g, first)
            out_of(2 * g + 1, second)
            return 0

        lax.fori_loop(0, n_rows // 2, hidden, 0)
        used.add((HIN, j))
        if j % 2:
            used.add((HOUT, j // 2))
        passed(4.5)
        if j % 2:
            half = j // 2
            write(pool.at[DG[half]], O_DH, saved[O_DH].at[:, half * 1024 : (half + 1) * 1024])
    write(xf, O_R3)
    for c in writes[7:]:
        c.wait()
    if gather is not None:
        gather.finish()


def forward(tokens, enc, dec_len, enc_len, arrays, remote):
    slots, width = tokens.shape
    hidden = arrays[1 + HIN].shape[-1]
    bottle = arrays[1 + DOWN].size // width * (NZ * NB if remote else 1)
    bf, f3 = functools.partial(jax.ShapeDtypeStruct, dtype=BF16), functools.partial(jax.ShapeDtypeStruct, dtype=F32)
    main = bf((slots, width))
    outs = [main] * 11 + [bf((slots, hidden)), bf((slots, bottle)), bf((slots, bottle)), f3((slots, width)), f3((2, slots, 128))]
    outs += [f3((width // PAIR, 2, slots)), f3((width // PAIR, 2, slots)), f3((16, width))]
    gathered = [bf((NZ, NB) + a.shape) for a in arrays] if remote else []
    params = dict(collective_id=0, has_side_effects=True) if remote else {}
    kept = pl.pallas_call(
        functools.partial(forward_kernel, remote),
        out_shape=gathered + outs,
        in_specs=[ANY, ANY, SMEM, SMEM] + [ANY] * len(arrays),
        out_specs=[ANY] * (len(gathered) + SAVED) + [WHOLE] * 3,
        scratch_shapes=[
            pltpu.VMEM((15, slots, width), BF16),
            pltpu.VMEM((slots, 2 * QB), F32),
            pltpu.VMEM((slots, 2 * QB), F32),
            pltpu.VMEM((slots, PAIR), BF16),
            pltpu.VMEM((slots, PAIR), BF16),
            pltpu.VMEM((16, slots), BF16),
            pltpu.VMEM((slots, width), F32),
            pltpu.VMEM((4, NZ, NB, 64, 1024), BF16),
            pltpu.VMEM((2, NB, 256, 1024), BF16),
            pltpu.VMEM((2, NZ, NB, bottle // 16, 1024), BF16),
            pltpu.VMEM((slots, bottle), BF16),
            pltpu.VMEM((slots, bottle), BF16),
            pltpu.VMEM((2, slots, 128), F32),
            pltpu.VMEM((NZ, NB, 32, 128), BF16),
            pltpu.VMEM((1, hidden), F32),
            pltpu.VMEM((1, bottle), F32),
            pltpu.SemaphoreType.DMA((3,)),
            pltpu.SemaphoreType.DMA((22,)),
            pltpu.SemaphoreType.DMA((24,)),
        ] + (gather_scratch([a.shape for a in arrays]) if remote else []),
        compiler_params=pltpu.CompilerParams(vmem_limit_bytes=VMEM, **params),
        cost_estimate=cost(slots * (16 * width * width + 4 * slots * width * 8), *arrays, *outs),
        name="forward",
    )(tokens, enc, dec_len, enc_len, *arrays)
    return (kept[: len(gathered)] or list(arrays)), kept[len(gathered) :]


def head_sums(grad_t, mix_t):
    product = grad_t.astype(F32) * mix_t.astype(F32)
    return jnp.sum(product.reshape(-1, HEAD, product.shape[1]), axis=1)


def head_back_kernel(dec_len, r3, cot, vec, db, ab, x2b, down, up, out, g3, g3b, grads, gbias):
    i = pl.program_id(0)
    ends = ends_of(dec_len)
    xhat, rstd = normalized(r3[...])
    gain = vec[G3 : G3 + 1, :]
    out[...] = (xhat * gain + vec[S3 : S3 + 1, :]).astype(BF16)
    pos = lax.broadcasted_iota(jnp.int32, r3.shape, 0) + i * r3.shape[0]
    upstream = jnp.where(pos < ends[2], cot[...].astype(F32), 0.0)
    g = norm_back(xhat, rstd, gain, upstream)
    g3b[...] = g.astype(BF16)
    g_adapt = (SCALE * g).astype(BF16)
    g_bottle = (db[...].astype(F32) * dot_nt(g_adapt, up[...])).astype(BF16)
    g3[...] = g + dot(g_bottle, down[...])

    @pl.when(i == 0)
    def _():
        grads[...] = jnp.zeros_like(grads)
        gbias[...] = jnp.zeros_like(gbias)

    grads[0] = grads[0] + dot_tn(g_bottle, x2b[...])
    grads[1] = grads[1] + dot_tn(ab[...], g_adapt)
    gbias[0:1, :] = gbias[0:1, :] + jnp.sum(g_adapt.astype(F32), axis=0, keepdims=True)
    wide = gbias[1:2, 0 : db.shape[1]]
    gbias[1:2, 0 : db.shape[1]] = wide + jnp.sum(g_bottle.astype(F32), axis=0, keepdims=True)


def full(shape):
    return pl.BlockSpec(shape, lambda *_: (0,) * len(shape))


def head_back(dec_len, r3, cot, vec, db, ab, x2b, down, up):
    slots, width = r3.shape
    bottle = db.shape[1]
    sds = jax.ShapeDtypeStruct
    row, low = pl.BlockSpec((RB, width), lambda i: (i, 0)), pl.BlockSpec((RB, bottle), lambda i: (i, 0))
    outs = [
        sds((slots, width), BF16), sds((slots, width), F32), sds((slots, width), BF16),
        sds((2, bottle, width), F32), sds((8, width), F32),
    ]
    return pl.pallas_call(
        head_back_kernel,
        grid=(slots // RB,),
        out_shape=outs,
        in_specs=[SMEM, row, row, full(vec.shape), low, low, row, full(down.shape), full(up.shape)],
        out_specs=[row] * 3 + [full(o.shape) for o in outs[3:]],
        compiler_params=pltpu.CompilerParams(vmem_limit_bytes=VMEM),
        cost_estimate=cost(slots * 4 * width * bottle, *outs, r3, cot),
        name="head_back",
    )(dec_len, r3, cot, vec, db, ab, x2b, down, up)


class Reduce:
    def __init__(self, grads, gbias, shares, bias, scratch):
        self.grads, self.gbias, self.shares, self.bias = grads, gbias, shares, bias
        (self.s1, self.r1, self.s2, self.r2, self.s3, self.r3, self.s4, self.r4, self.f5, self.r5,
         self.sb, self.rb, self.acc2, self.acc3, self.send, self.recv) = scratch
        self.core, t = lax.axis_index("grp"), lax.axis_index("tok")
        self.z, b = t // NB, t % NB
        self.y, self.x = b // 2, b % 2
        self.b = b
        by_x, by_y = self.y * 2 + (1 - self.x), (1 - self.y) * 2 + self.x
        core, z = self.core, self.z
        n2, n3 = by_x + core * (by_y - by_x), by_y + core * (by_x - by_y)
        self.across = {"grp": 1 - core, "tok": t}
        self.second = {"grp": core, "tok": z * NB + n2}
        self.third = {"grp": core, "tok": z * NB + n3}
        self.along = [{"grp": core, "tok": (z + d) % NZ * NB + b} for d in (1, 2, 3)]

    def copy(self, n, src, dst, to):
        return pltpu.make_async_remote_copy(src, dst, self.send.at[n], self.recv.at[n], device_id=to, device_id_type=MESH)

    def copies(self, stage):
        if stage == 1:
            return [self.copy(0, self.s1, self.r1, self.across), self.copy(1, self.sb.at[0], self.rb.at[0], self.across)]
        if stage == 2:
            return [self.copy(2, self.s2, self.r2, self.second), self.copy(3, self.sb.at[1], self.rb.at[1], self.second)]
        if stage == 3:
            return [self.copy(4, self.s3, self.r3, self.third), self.copy(5, self.sb.at[2], self.rb.at[2], self.third)]
        if stage == 4:
            moves = [self.copy(6 + d, self.s4.at[d], self.r4.at[d], self.along[d]) for d in range(3)]
            return moves + [self.copy(9 + d, self.sb.at[3], self.rb.at[3 + d], self.along[d]) for d in range(3)]
        return [self.copy(12, self.f5, self.r5, self.across)]

    def go(self, stage):
        for c in self.copies(stage):
            c.start()

    def wait(self, stage):
        for c in self.copies(stage):
            c.wait()

    def begin(self):
        sem = pltpu.get_barrier_semaphore()
        for peer in [self.across, self.second, self.third, *self.along]:
            pl.semaphore_signal(sem, inc=1, device_id=peer, device_id_type=MESH)
        pl.semaphore_wait(sem, 6)
        self.s1[...] = self.grads[1 - self.core].astype(BF16)
        self.bias[...] = jnp.concatenate([self.gbias[...], jnp.zeros_like(self.gbias[...])], axis=0)
        self.sb[0] = self.bias[...].astype(BF16)
        self.go(1)

    def add_bias(self, n, more):
        self.bias[...] = self.bias[...] + more
        self.sb[n] = self.bias[...].astype(BF16)

    def first(self):
        self.wait(1)
        total = self.grads[self.core] + self.r1[...].astype(F32)
        rows, width = total.shape[0] // (NZ * NB), total.shape[1]
        total = total.reshape(NZ, 2, 2, rows, width)
        by_x = [total[:, :, k].reshape(2 * NZ, rows, width) for k in range(2)]
        by_y = [total[:, k].reshape(2 * NZ, rows, width) for k in range(2)]
        even, odd = [jnp.where(self.core == 0, u, v) for u, v in zip(by_x, by_y)]
        high = jnp.where(self.core == 0, self.x, self.y) == 1
        self.acc2[...] = jnp.where(high, odd, even)
        self.s2[...] = jnp.where(high, even, odd).astype(BF16)
        self.add_bias(1, self.rb[0].astype(F32))
        self.go(2)

    def next(self):
        self.wait(2)
        total = self.acc2[...] + self.r2[...].astype(F32)
        total = total.reshape((NZ, 2) + total.shape[1:])
        high = jnp.where(self.core == 0, self.y, self.x) == 1
        self.acc3[...] = jnp.where(high, total[:, 1], total[:, 0])
        self.s3[...] = jnp.where(high, total[:, 0], total[:, 1]).astype(BF16)
        self.add_bias(2, self.rb[1].astype(F32))
        self.go(3)

    def then(self):
        self.wait(3)
        self.acc3[...] = self.acc3[...] + self.r3[...].astype(F32)
        for d in range(3):
            self.s4[d] = self.acc3[(self.z + d + 1) % NZ].astype(BF16)
        self.add_bias(3, self.rb[2].astype(F32))
        self.go(4)

    def last(self):
        self.wait(4)
        total = self.acc3[self.z]
        for d in range(3):
            total = total + self.r4[d].astype(F32)
        self.bias[...] = self.bias[...] + self.rb[3].astype(F32) + self.rb[4].astype(F32) + self.rb[5].astype(F32)
        self.f5[...] = total
        self.shares[self.core] = total
        self.go(5)

    def end(self):
        self.wait(5)
        self.shares[1 - self.core] = self.r5[...]


def reduce_scratch(bottle, width):
    vmem, rows = pltpu.VMEM, bottle // (NZ * NB)
    pairs = [(NZ * NB,), (2 * NZ,), (NZ,), (3,)]
    bufs = [vmem((bottle, width), BF16)] * 2
    for lead in pairs[1:]:
        bufs += [vmem(lead + (rows, width), BF16)] * 2
    bufs += [vmem((rows, width), F32)] * 2
    bufs += [vmem((4, 16, width), BF16), vmem((6, 16, width), BF16)]
    bufs += [vmem((2 * NZ, rows, width), F32), vmem((NZ, rows, width), F32)]
    return bufs + [pltpu.SemaphoreType.DMA((13,))] * 2


def ffn_back_kernel(remote, vec, g3b, dh, w_out, w_in, grads, gbias, g3, xh2, stat, cm, co, gr2, gmix, delta, shares, bias,
                    acc, g3_v, xh2_v, stat_v, cm_v, co_v, sems, *scratch):
    step = pl.program_id(0)
    n_rows = g3b.shape[0] // RB
    if remote:
        reduce = Reduce(grads, gbias, shares, bias, scratch)
        for n, part in enumerate((reduce.begin, reduce.first, reduce.next, reduce.then)):
            pl.when(step == n)(part)
    moves = [(g3, g3_v), (xh2, xh2_v), (stat, stat_v), (cm, cm_v), (co, co_v)]
    copies = [pltpu.make_async_copy(a, b, sems.at[n]) for n, (a, b) in enumerate(moves)]

    @pl.when(step == 0)
    def _():
        for c in copies:
            c.start()
        acc[...] = jnp.zeros_like(acc)

    def hidden(i, _):
        blocks = [rows_of(2 * i), rows_of(2 * i + 1)]
        pres = [dot_nt(g3b[rows, :], w_out[...]) for rows in blocks]
        for rows, pre in zip(blocks, pres):
            g = (dh[rows, :].astype(F32) * pre).astype(BF16)
            acc[rows, :] = acc[rows, :] + dot_nt(g, w_in[...])
        return 0

    lax.fori_loop(0, n_rows // 2, hidden, 0)

    @pl.when(step == pl.num_programs(0) - 1)
    def _():
        if remote:
            reduce.last()
        for c in copies:
            c.wait()

        def last(i, _):
            rows = rows_of(i)
            g = acc[rows, :] + g3_v[rows, :]
            g = norm_back(xh2_v[rows, :].astype(F32), stat_v[1, rows, 0:1], vec[G2 : G2 + 1, :], g)
            gr2[rows, :] = g
            mix = dot_nt(co_v[...], g.astype(BF16)).astype(BF16)
            gmix[:, rows] = mix
            delta[:, rows] = head_sums(mix, cm_v[:, rows])
            return 0

        lax.fori_loop(0, n_rows, last, 0)
        if remote:
            reduce.end()


def ffn_back(remote, vec, g3b, dh, w_out, w_in, grads, gbias, g3, xh2, stat, cm, co):
    slots, width = g3.shape
    hidden = dh.shape[1]
    step = 1024
    sds = jax.ShapeDtypeStruct
    bottle = grads.shape[1]
    outs = [sds((slots, width), F32), sds((width, slots), BF16), sds((width // HEAD, slots), F32)]
    outs += [sds((2, bottle // (NZ * NB), width), F32), sds((16, width), F32)]
    late = [g3, xh2, stat, cm, co]
    params = dict(collective_id=1, has_side_effects=True) if remote else {}
    return pl.pallas_call(
        functools.partial(ffn_back_kernel, remote),
        grid=(hidden // step,),
        out_shape=outs,
        in_specs=[
            full(vec.shape), full(g3b.shape),
            pl.BlockSpec((slots, step), lambda c: (0, c)),
            pl.BlockSpec((step, width), lambda c: (c, 0)),
            pl.BlockSpec((width, step), lambda c: (0, c)),
            full(grads.shape), full(gbias.shape),
        ] + [ANY] * len(late),
        out_specs=[full(o.shape) for o in outs],
        scratch_shapes=[pltpu.VMEM((slots, width), F32)]
        + [pltpu.VMEM(a.shape, a.dtype) for a in late]
        + [pltpu.SemaphoreType.DMA((len(late),))]
        + (reduce_scratch(bottle, width) if remote else []),
        compiler_params=pltpu.CompilerParams(vmem_limit_bytes=VMEM, **params),
        cost_estimate=cost(slots * width * (2 * hidden + width), *outs, dh, w_out, w_in, co),
        name="ffn_back",
    )(vec, g3b, dh, w_out, w_in, grads, gbias, *late)


def cross_tail(i, dq, dk, dv, vec, gr2, xh1, stat, sm, cq, ck, cv, so, genc, gmix, delta):
    rows = rows_of(i)
    genc[rows, :] = (dot_nt(dk[rows, :], ck[...]) + dot_nt(dv[rows, :], cv[...])).astype(BF16)
    g = gr2[rows, :] + dot_nt(dq[rows, :], cq[...])
    g = norm_back(xh1[rows, :].astype(F32), stat[0, rows, 0:1], vec[G1 : G1 + 1, :], g)
    gr2[rows, :] = g
    mix = dot_nt(so[...], g.astype(BF16)).astype(BF16)
    gmix[:, rows] = mix
    delta[:, rows] = head_sums(mix, sm[:, rows])


def self_tail(i, dq, dk, dv, gr1, sq, sk, sv, gtok):
    rows = rows_of(i)
    g = gr1[rows, :] + dot_nt(dq[rows, :], sq[...]) + dot_nt(dk[rows, :], sk[...]) + dot_nt(dv[rows, :], sv[...])
    gtok[rows, :] = g.astype(BF16)


def attend_back_kernel(causal, q_len, k_len, q_t, k, v, g_t, lse, delta, *rest):
    if causal:
        late, outs, rest = rest[:4], rest[4:5], rest[5:]
        late_v, staged, rest = rest[:4], rest[4:5], rest[5:]
    else:
        vec, late, outs, new_delta, rest = rest[0], rest[1:9], rest[9:12], rest[12], rest[13:]
        late_v, staged, rest = rest[:8], rest[8:10], rest[10:]
    (dq, dk, dv, late_s, out_s, dk_t, dv_t, dq_t, k_t, qx, gx, kf, s_buf, d_buf, tile_i, tile_j, new_q, new_k, tiles) = rest
    step = pl.program_id(0)

    @pl.when(step == 0)
    def _():
        for n, (src, dst) in enumerate(zip(late, late_v)):
            pltpu.make_async_copy(src, dst, late_s.at[n]).start()

    slots, pairs = k.shape[0], k.shape[1] // PAIR
    blocks = slots // QB
    q_ends, k_ends = ends_of(q_len), ends_of(k_len)

    @pl.when(pl.program_id(0) == 0)
    def _():
        key_features(kf, k_ends)
        count = jnp.int32(0)
        reached = jnp.int32(0)
        for i in range(blocks):
            low, _ = pick(segment(jnp.int32(i * QB), q_ends), k_ends, 0, slots)
            _, high = pick(segment(jnp.int32(i * QB + QB - 1), q_ends), k_ends, 0, slots)
            if causal:
                high = jnp.minimum(high, (i + 1) * QB)

            def put(j, n, i=i, low=low, reached=reached):
                tile_i[n] = i
                tile_j[n] = j
                new_q[n] = (j == low // QB).astype(jnp.int32)
                new_k[n] = (j >= reached).astype(jnp.int32)
                return n + 1

            count = lax.fori_loop(low // QB, (high + QB - 1) // QB, put, count)
            reached = jnp.maximum(reached, (high + QB - 1) // QB)
        tiles[0] = count

    k_t[...] = jnp.transpose(k[...])
    empty = jnp.zeros((PAIR - 16, 2 * QB), BF16)
    for i in range(blocks):
        cols = slice(i * QB, (i + 1) * QB)
        far = twice(query_features(i * QB, QB, q_ends))
        for n in range(pairs):
            part = slice(n * PAIR, (n + 1) * PAIR)
            both_lse = jnp.concatenate([lse[n, 0:1, cols], lse[n, 1:2, cols]], axis=1)
            both_delta = jnp.concatenate([delta[2 * n : 2 * n + 1, cols], delta[2 * n + 1 : 2 * n + 2, cols]], axis=1)
            qx[n, i, :PAIR, :] = two_heads(q_t[part, cols])
            qx[n, i, PAIR : PAIR + 16, :] = (far + in_parts(-both_lse, 4)).astype(BF16)
            qx[n, i, PAIR + 16 :, :] = empty
            gx[n, i, :PAIR, :] = two_heads(g_t[part, cols])
            gx[n, i, PAIR : PAIR + 16, :] = in_parts(-both_delta, 4).astype(BF16)
            gx[n, i, PAIR + 16 :, :] = empty

    if causal:
        shape = (QB, 2 * QB)
        ahead = lax.broadcasted_iota(jnp.int32, shape, 0) - lax.broadcasted_iota(jnp.int32, shape, 1) % QB

    def keys_of(j):
        return pl.ds(pl.multiple_of(j * QB, QB), QB)

    def scores(t, n):
        i, keys = tile_i[t], keys_of(tile_j[t])
        part = slice(n * PAIR, (n + 1) * PAIR)
        s_buf[n] = dot(jnp.concatenate([k[keys, part], kf[keys, :]], axis=1), qx[n, i])
        d_buf[n] = dot(jnp.concatenate([v[keys, part], kf[keys, :]], axis=1), gx[n, i])

    def grads(t, n):
        i, j = tile_i[t], tile_j[t]
        keys = keys_of(j)
        p = jnp.exp(s_buf[n])
        if causal:
            p = jnp.where(ahead <= (i - j) * QB, p, 0.0)
        d = (p * d_buf[n]).astype(BF16)
        first_q, first_k = new_q[t] == 1, new_k[t] == 1
        dv_t[n, :, keys] = jnp.where(first_k, 0.0, dv_t[n, :, keys]) + dot_nt(gx[n, i, :PAIR, :], p.astype(BF16))
        dk_t[n, :, keys] = jnp.where(first_k, 0.0, dk_t[n, :, keys]) + dot_nt(qx[n, i, :PAIR, :], d)
        dq_t[n, i] = jnp.where(first_q, 0.0, dq_t[n, i]) + dot(k_t[n * PAIR : (n + 1) * PAIR, keys], d)

    def loop(t, _):
        for n in range(pairs):
            grads(t - 1, n)
            scores(t, n)
        return 0

    last = tiles[0]
    for n in range(pairs):
        scores(0, n)
    lax.fori_loop(1, last, loop, 0)
    for n in range(pairs):
        grads(last - 1, n)
    for n in range(pairs):
        part = pl.ds(pl.multiple_of((step * pairs + n) * PAIR, PAIR), PAIR)
        dk[:, part] = jnp.transpose(dk_t[n].astype(BF16))
        dv[:, part] = jnp.transpose(dv_t[n].astype(BF16))
        for i in range(blocks):
            dq[i * QB : (i + 1) * QB, part] = jnp.transpose((one_of_each(dq_t[n, i]) * HEAD ** (-0.5)).astype(BF16))

    @pl.when(step == pl.num_programs(0) - 1)
    def _():
        for n, (src, dst) in enumerate(zip(late, late_v)):
            pltpu.make_async_copy(src, dst, late_s.at[n]).wait()
        results = [*staged] if causal else [staged[0], late_v[0], staged[1]]

        def back(n, i):
            at = (slice(None), rows_of(i)) if n == 2 else (rows_of(i), slice(None))
            return pltpu.make_async_copy(results[n].at[at], outs[n].at[at], out_s.at[n, i])

        def tail(i, _):
            if causal:
                self_tail(i, dq, dk, dv, *late_v, staged[0])
            else:
                cross_tail(i, dq, dk, dv, vec, *late_v, *staged, new_delta)
            for n in range(len(outs)):
                back(n, i).start()
            return 0

        lax.fori_loop(0, slots // RB, tail, 0)
        for i in range(slots // RB):
            for n in range(len(outs)):
                back(n, i).wait()


def attend_back(causal, q_len, k_len, q_t, k, v, g_t, lse, delta, vec, late, group=4):
    slots, width = k.shape
    pairs, blocks, heads = width // PAIR, slots // QB, width // HEAD
    col = pl.BlockSpec((slots, group * PAIR), lambda p: (0, p))
    row = pl.BlockSpec((group * PAIR, slots), lambda p: (p, 0))
    stat = pl.BlockSpec((group, 2, slots), lambda p: (p, 0, 0))
    vmem, sds = pltpu.VMEM, jax.ShapeDtypeStruct
    outs, specs, staged = [sds((slots, width), BF16)], [ANY], [vmem((slots, width), BF16)]
    extra, extra_specs = [], []
    if not causal:
        outs += [sds((slots, width), F32), sds((width, slots), BF16), sds((heads, slots), F32)]
        specs += [ANY, ANY, full((heads, slots))]
        staged += [vmem((width, slots), BF16)]
        extra, extra_specs = [vec], [full(vec.shape)]
    return pl.pallas_call(
        functools.partial(attend_back_kernel, causal),
        grid=(pairs // group,),
        out_shape=outs,
        in_specs=[SMEM, SMEM, row, col, col, row, stat, pl.BlockSpec((2 * group, slots), lambda p: (p, 0))]
        + extra_specs + [ANY] * len(late),
        out_specs=specs,
        scratch_shapes=[vmem(a.shape, a.dtype) for a in late] + staged + [
            vmem((slots, width), BF16),
            vmem((slots, width), BF16),
            vmem((slots, width), BF16),
            pltpu.SemaphoreType.DMA((len(late),)),
            pltpu.SemaphoreType.DMA((3, slots // RB)),
            vmem((group, PAIR, slots), F32),
            vmem((group, PAIR, slots), F32),
            vmem((group, blocks, PAIR, 2 * QB), F32),
            vmem((group * PAIR, slots), BF16),
            vmem((group, blocks, 2 * PAIR, 2 * QB), BF16),
            vmem((group, blocks, 2 * PAIR, 2 * QB), BF16),
            vmem((slots, PAIR), BF16),
            vmem((group, QB, 2 * QB), F32),
            vmem((group, QB, 2 * QB), F32),
            pltpu.SMEM((blocks * blocks,), jnp.int32),
            pltpu.SMEM((blocks * blocks,), jnp.int32),
            pltpu.SMEM((blocks * blocks,), jnp.int32),
            pltpu.SMEM((blocks * blocks,), jnp.int32),
            pltpu.SMEM((1,), jnp.int32),
        ],
        compiler_params=pltpu.CompilerParams(vmem_limit_bytes=VMEM),
        cost_estimate=cost(5 * slots * slots * width * 4 + 4 * slots * width * width, k, v, k, v, *late),
        name="self_back" if causal else "cross_back",
    )(q_len, k_len, q_t, k, v, g_t, lse, delta, *extra, *late)


def local(groups, tokens, enc, dec_len, enc_len, cot, sq, sqb, sk, sv, svb, so, sob, g1, s1, cq, cqb, ck, cv, cvb, co, cob,
          g2, s2, hin, hinb, hout, houtb, g3, s3, down, downb, up, upb):
    vectors = (sqb, svb, sob, g1, s1, cqb, cvb, cob, g2, s2, houtb, g3, s3, upb)
    weights = (sq, sk, sv, ck, cv, so, cq, co, down, up, hout, hin)
    remote = groups == NZ * NB
    if remote:
        arrays = [pack_vectors(vectors, hinb, downb, 1)[0], *weights]
    else:
        every = functools.partial(lax.all_gather, axis_name="tok", axis=0, tiled=True)
        packed = pack_vectors([every(v) for v in vectors], every(hinb), every(downb), NZ * NB)
        arrays = [packed.reshape(NZ, NB, 32, 128)]
        arrays += [every(w).reshape(NZ, NB, w.shape[0] * groups // (NZ * NB), w.shape[1]) for w in weights]
    arrays, kept = forward(tokens, enc, dec_len, enc_len, arrays, remote)
    flat = [a.reshape(-1, a.shape[-1]) for a in arrays[1:]]
    lse1, lse2, vec = kept[SAVED:]
    out, g3, g3b, grads, gbias = head_back(
        dec_len, kept[O_R3], cot, vec, kept[O_DB], kept[O_AB], kept[O_X2B], flat[DOWN], flat[UP]
    )
    _, bottle, width = grads.shape
    if not remote:
        parts = [grads[0].reshape(groups, -1, width), grads[1].reshape(groups, -1, width), jnp.broadcast_to(gbias[None], (groups, 8, width))]
        share = lax.psum_scatter(jnp.concatenate(parts, axis=1).astype(BF16), "tok", scatter_dimension=0, tiled=False)
    gr2, gmix, delta, shares, bias = ffn_back(
        remote, vec, g3b, kept[O_DH], flat[HOUT], flat[HIN], grads, gbias, g3, kept[O_XH2], kept[O_STAT], kept[O_CM], flat[CO]
    )
    genc, gr1, gmix, delta = attend_back(
        False, dec_len, enc_len, kept[O_CQ], kept[O_CK], kept[O_CV], gmix, lse2, delta, vec,
        (gr2, kept[O_XH1], kept[O_STAT], kept[O_SM], flat[CQ], flat[CK], flat[CV], flat[SO]),
    )
    (gtok,) = attend_back(
        True, dec_len, dec_len, kept[O_SQ], kept[O_SK], kept[O_SV], gmix, lse1, delta, vec,
        (gr1, flat[SQ], flat[SK], flat[SV]),
    )
    rows = bottle // groups
    if not remote:
        total = lax.psum(share, "grp").astype(F32)
        shares, bias = total[: 2 * rows].reshape(2, rows, width), total[2 * rows :]
    me = lax.axis_index("tok")
    up_bias = lax.dynamic_slice(bias[0], (me * (width // groups),), (width // groups,))
    down_bias = lax.dynamic_slice(bias[1], (me * rows,), (rows,))
    return out, gtok, genc, shares[0], down_bias, shares[1], up_bias


def solution(mesh):
    split = P(("grp", "tok"), None)
    two, one = P("tok", None), P("tok")
    ranks = [2, 1, 2, 2, 1, 2, 1, 1, 1, 2, 1, 2, 2, 1, 2, 1, 1, 1, 2, 1, 2, 1, 1, 1, 2, 1, 2, 1]
    return jax.shard_map(
        functools.partial(local, mesh.shape["tok"]),
        mesh=mesh,
        in_specs=(split,) * 5 + tuple(two if r == 2 else one for r in ranks),
        out_specs=(split,) * 3 + (two, one, two, one),
        check_vma=False,
    )
```

```python
import functools

import jax
import jax.numpy as jnp
from jax import lax
from jax.experimental import pallas as pl
from jax.experimental.pallas import tpu as pltpu
from jax.sharding import PartitionSpec as P

F32 = jnp.float32
BF16 = jnp.bfloat16
HEAD = 64
PAIR = 2 * HEAD
EPSILON = 1e-05
SCALE = 4.0
RB = 256
QB = 128
KB = 256
FAR = float(1 << 30)
MIB = 1 << 20
VMEM = 62 * MIB
MESH = pl.DeviceIdType.MESH
ANY = pl.BlockSpec(memory_space=pl.ANY)
SMEM = pl.BlockSpec(memory_space=pltpu.SMEM)
WHOLE = pl.BlockSpec(memory_space=pltpu.VMEM)


def dot(a, b):
    return jnp.dot(a, b, preferred_element_type=F32)


def dot_nt(a, b):
    return lax.dot_general(a, b, (((1,), (1,)), ((), ())), preferred_element_type=F32)


def dot_tn(a, b):
    return lax.dot_general(a, b, (((0,), (0,)), ((), ())), preferred_element_type=F32)


def cost(macs, *arrays):
    return pl.CostEstimate(flops=2 * macs, bytes_accessed=sum(a.size * a.dtype.itemsize for a in arrays), transcendentals=0)


def rows_of(i):
    return pl.ds(pl.multiple_of(i * RB, RB), RB)


def lanes_of(p):
    return pl.ds(pl.multiple_of(p * PAIR, PAIR), PAIR)


def two_heads(values):
    row = lax.broadcasted_iota(jnp.int32, values.shape, 0)
    zero = jnp.zeros_like(values)
    return jnp.concatenate([jnp.where(row < HEAD, values, zero), jnp.where(row < HEAD, zero, values)], axis=1)


def one_of_each(values):
    n = values.shape[1] // 2
    row = lax.broadcasted_iota(jnp.int32, (values.shape[0], n), 0)
    return jnp.where(row < HEAD, values[:, :n], values[:, n:])


def twice(values):
    return jnp.concatenate([values, values], axis=1)


def normalized(r):
    centred = r - jnp.mean(r, axis=-1, keepdims=True)
    rstd = lax.rsqrt(jnp.mean(centred * centred, axis=-1, keepdims=True) + EPSILON)
    return centred * rstd, rstd


def norm_back(xhat, rstd, gain, upstream):
    u = upstream * gain
    first = jnp.mean(u, axis=-1, keepdims=True)
    second = jnp.mean(u * xhat, axis=-1, keepdims=True)
    return (u - first - xhat * second) * rstd


def gelu_parts(v):
    size = jnp.abs(v)
    bell = jnp.exp(-0.5 * v * v)
    t = 1.0 / (1.0 + 0.23164188 * size)
    poly = t * (0.127414796 + t * (-0.142248368 + t * (0.71070687 + t * (-0.726576013 + t * 0.530702714))))
    tail = poly * bell
    phi = jnp.where(v < 0, tail, 1.0 - tail)
    return v * phi, phi + (0.3989422804014327 * v) * bell


def ends_of(ref):
    e0 = ref[0, 0]
    e1 = e0 + ref[0, 1]
    return e0, e1, e1 + ref[0, 2]


def segment(position, ends):
    return sum((position >= e).astype(jnp.int32) for e in ends)


def key_features(ref, ends):
    def block(i, _):
        shape = (RB, ref.shape[1])
        seg = segment(lax.broadcasted_iota(jnp.int32, shape, 0) + i * RB, ends)
        lane = lax.broadcasted_iota(jnp.int32, shape, 1)
        ref[rows_of(i), :] = ((lane == seg) | ((lane >= 4) & (lane < 7))).astype(F32).astype(BF16)
        return 0

    lax.fori_loop(0, ref.shape[0] // RB, block, 0)


def query_features(first, count, ends):
    seg = segment(lax.broadcasted_iota(jnp.int32, (16, count), 1) + first, ends)
    row = lax.broadcasted_iota(jnp.int32, (16, count), 0)
    return jnp.where((row < 4) & (row != seg), -FAR, 0.0)


def in_parts(values, row):
    at = lax.broadcasted_iota(jnp.int32, (16, values.shape[1]), 0)
    high = values.astype(BF16).astype(F32)
    middle = (values - high).astype(BF16).astype(F32)
    low = values - high - middle
    return jnp.where(at == row, high, jnp.where(at == row + 1, middle, jnp.where(at == row + 2, low, 0.0)))


def pick(seg, ends, first, last):
    e0, e1, e2 = ends
    start = jnp.where(seg == 0, first, jnp.where(seg == 1, e0, jnp.where(seg == 2, e1, e2)))
    stop = jnp.where(seg == 0, e0, jnp.where(seg == 1, e1, jnp.where(seg == 2, e2, last)))
    return start, stop


NZ, NB = 4, 4
WEIGHTS = 12
SQ, SK, SV, CK, CV, SO, CQ, CO, DOWN, UP, HOUT, HIN = range(WEIGHTS)
VEC = 0
HALVED = (SQ, SK, SV)


def pieces(shapes):
    found = []
    for a, (rows, cols) in enumerate(shapes):
        if rows >= 256:
            found += [(a, j, 4, 0, 1, j > 1) for j in range(4)]
        elif cols >= 4096:
            found += [(a, 0, 1, j, 8, True) for j in range(8)]
        elif a == 1 + SQ:
            found += [(1 + w, 0, 1, h, 2, False) for h in range(2) for w in HALVED]
        elif a - 1 not in HALVED:
            found.append((a, 0, 1, 0, 1, False))
    return found


class Gather:
    RATE = 0.086

    def __init__(self, ins, outs, stages, sems):
        self.ins, self.outs, self.stages = ins, outs, stages
        self.in_s, self.own_s, self.zs, self.zr, self.ws, self.wr, self.ps, self.pr = sems
        self.core, t = lax.axis_index("grp"), lax.axis_index("tok")
        self.z, b = t // NB, t % NB
        y, x = b // 2, b % 2
        by_x, by_y = y * 2 + (1 - x), (1 - y) * 2 + x
        self.b = b
        self.n2 = by_x + self.core * (by_y - by_x)
        self.n3 = by_y + self.core * (by_x - by_y)
        self.pieces = pieces([r.shape for r in ins])
        count = len(self.pieces)
        self.size = []
        for a, _, rn, _, cn, _ in self.pieces:
            rows, cols = ins[a].shape
            self.size.append(NZ * NB * rows * cols * 2 / (rn * cn) / MIB)
        self.now, self.short, self.swaps, self.long = 5.0, 5.0, 0.0, 8.0
        self.next = [0] * 5
        self.detour = [i for i in range(count) if self.pieces[i][5]]
        self.arrive = {}

    def dev(self, core, z, b):
        return {"grp": core, "tok": z * NB + b}

    def peers(self):
        c, z, b = self.core, self.z, self.b
        along = [self.dev(c, (z + d) % NZ, b) for d in (1, 2, 3)]
        return along + [self.dev(c, z, self.n2), self.dev(c, z, self.n3), self.dev(1 - c, z, b)]

    def barrier(self):
        sem = pltpu.get_barrier_semaphore()
        peers = self.peers()
        for p in peers:
            pl.semaphore_signal(sem, inc=1, device_id=p, device_id_type=MESH)
        pl.semaphore_wait(sem, len(peers))

    def cut(self, i):
        a, rj, rn, cj, cn, _ = self.pieces[i]
        rows, cols = self.ins[a].shape
        r, c = rows // (2 * rn), cols // cn
        first = pl.multiple_of(self.core * (rows // 2) + rj * r, r)
        return a, pl.ds(first, r), pl.ds(rj * r, r), pl.ds(cj * c, c)

    def half(self, a):
        rows = self.ins[a].shape[0] // 2
        return pl.ds(pl.multiple_of(self.core * rows, rows), rows)

    def staged(self, a):
        return pltpu.make_async_copy(self.ins[a].at[self.half(a)], self.stages[a], self.in_s.at[a])

    def own(self, a):
        return pltpu.make_async_copy(self.stages[a], self.outs[a].at[self.z, self.b, self.half(a)], self.own_s.at[a])

    def along_z(self, i, d):
        a, r, here, c = self.cut(i)
        return pltpu.make_async_remote_copy(
            self.stages[a].at[here, c], self.outs[a].at[self.z, self.b, r, c],
            self.zs.at[i, d - 1], self.zr.at[i, d - 1],
            device_id=self.dev(self.core, (self.z + d) % NZ, self.b), device_id_type=MESH,
        )

    def aside(self, i):
        a, r, here, c = self.cut(i)
        return pltpu.make_async_remote_copy(
            self.stages[a].at[here, c], self.outs[a].at[self.z, self.b, r, c], self.ps.at[i, 0], self.pr.at[i, 0],
            device_id=self.dev(self.core, self.z, self.n2), device_id_type=MESH,
        )

    def along_z_too(self, i, d):
        a, r, _, c = self.cut(i)
        ref = self.outs[a].at[self.z, self.n2, r, c]
        return pltpu.make_async_remote_copy(
            ref, ref, self.ws.at[i, d - 1], self.wr.at[i, d - 1],
            device_id=self.dev(self.core, (self.z + d) % NZ, self.b), device_id_type=MESH,
        )

    def column(self, i, b, k, to):
        a, r, _, c = self.cut(i)
        ref = self.outs[a].at[:, b, r, c]
        return pltpu.make_async_remote_copy(
            ref, ref, self.ps.at[i, k], self.pr.at[i, k],
            device_id=self.dev(self.core, self.z, to), device_id_type=MESH,
        )

    def second(self, i):
        return self.column(i, self.b, 0, self.n2)

    def third(self, i):
        return self.column(i, self.b, 1, self.n3)

    def onward(self, i):
        return self.column(i, self.n2, 2, self.n3)

    def swap(self, i):
        a, r, _, c = self.cut(i)
        ref = self.outs[a].at[:, :, r, c]
        return pltpu.make_async_remote_copy(
            ref, ref, self.ps.at[i, 3], self.pr.at[i, 3],
            device_id=self.dev(1 - self.core, self.z, self.b), device_id_type=MESH,
        )

    def begin(self):
        here = set()
        for i, piece in enumerate(self.pieces):
            if piece[0] not in here:
                here.add(piece[0])
                self.staged(piece[0]).wait()
                self.own(piece[0]).start()
            for d in (1, 2, 3):
                self.along_z(i, d).start()
            self.long += self.size[i] / 4 / self.RATE
            self.arrive["z", i] = self.long
            if piece[5]:
                self.aside(i).start()
                self.short += self.size[i] / 32 / self.RATE
                self.arrive["aside", i] = self.short + 1

    def ready(self, kind):
        at = self.next[kind]
        if kind == 4:
            return self.arrive["aside", self.detour[at]] if at < len(self.detour) else None
        if at >= len(self.pieces):
            return None
        names = (("z",), ("z2",) if self.pieces[at][5] else ("second",), ("third", "onward"), ("swap",))[kind]
        when = [self.arrive.get((name, at)) for name in names]
        return None if None in when else max(when)

    def event(self, kind):
        self.now = max(self.now, self.ready(kind)) + 0.15
        at = self.next[kind]
        self.next[kind] += 1
        i = self.detour[at] if kind == 4 else at
        a, rj, _, cj, _, detour = self.pieces[i]
        link = self.size[i] / 8 / self.RATE

        def sent(name):
            self.short = max(self.short, self.now) + link
            self.arrive[name, i] = self.short + 1

        if kind == 0:
            if rj == 0 and cj == 0:
                self.own(a).wait()
            for d in (1, 2, 3):
                self.along_z(i, d).wait_recv()
            if not detour:
                self.second(i).start()
                sent("second")
            self.third(i).start()
            sent("third")
        elif kind == 1:
            if detour:
                for d in (1, 2, 3):
                    self.along_z_too(i, d).wait_recv()
            else:
                self.second(i).wait_recv()
            self.onward(i).start()
            sent("onward")
        elif kind == 2:
            self.third(i).wait_recv()
            self.onward(i).wait_recv()
            self.swap(i).start()
            self.swaps = max(self.swaps, self.now) + self.size[i] * 0.86
            self.arrive["swap", i] = self.swaps + 1.5
        elif kind == 3:
            self.swap(i).wait_recv()
        else:
            self.aside(i).wait_recv()
            for d in (1, 2, 3):
                self.along_z_too(i, d).start()
            self.long = max(self.long, self.now) + self.size[i] / 4 / self.RATE
            self.arrive["z2", i] = self.long

    def pump(self):
        going = True
        while going:
            going = False
            for kind in (4, 1, 2, 3, 0):
                when = self.ready(kind)
                if when is not None and when <= self.now and (kind or self.short - self.now < 7):
                    self.event(kind)
                    going = True
                    break

    def passed(self, us):
        self.now += us
        self.pump()

    def until(self, last):
        while self.next[3] <= last:
            self.pump()
            if self.next[3] <= last:
                late = [(self.ready(k) + (max(0, self.short - self.now - 7) if k == 0 else 0), -k) for k in range(5) if self.ready(k) is not None]
                self.event(-min(late)[1])

    def whole(self, a):
        self.until(max(i for i, p in enumerate(self.pieces) if p[0] == a))

    def part(self, a, j):
        self.until([i for i, p in enumerate(self.pieces) if p[0] == a][j])

    def finish(self):
        self.until(len(self.pieces) - 1)
        for i, piece in enumerate(self.pieces):
            for d in (1, 2, 3):
                self.along_z(i, d).wait_send()
                if piece[5]:
                    self.along_z_too(i, d).wait_send()
            for copy in (self.aside if piece[5] else self.second, self.third, self.onward, self.swap):
                copy(i).wait_send()


def gather_scratch(shapes):
    n, k = len(shapes), len(pieces(shapes))
    dma = pltpu.SemaphoreType.DMA
    return [pltpu.VMEM((r // 2, c), BF16) for r, c in shapes] + [dma((n,)), dma((n,)), dma((k, 3)), dma((k, 3)), dma((k, 3)), dma((k, 3)), dma((k, 4)), dma((k, 4))]


SQB, SVB, SOB, G1, S1, CQB, CVB, COB, G2, S2, HOB, G3, S3, AUB = ((p % 2) * 8 + p // 2 for p in range(14))


def pack_vectors(vectors, hidden_bias, down_bias, groups):
    total, at = 0, 0
    for v in (*vectors, hidden_bias, down_bias):
        part = v.reshape(groups, -1) if groups > 1 else v
        more = part.shape[-1]
        total = total + jnp.pad(part, [(0, 0)] * (part.ndim - 1) + [(at, 4096 - at - more)])
        at += more
    return total.reshape(groups, 32, 128)


def unpack_vectors(packed, vec, hidden_bias, down_bias):
    lane = lax.broadcasted_iota(jnp.int32, (16, 128), 1)
    blocks = [packed[t][:16].astype(F32) for t in range(16)]
    turned = [pltpu.roll(b, HEAD, 1) for b in blocks]
    for u in range(8):
        cols = slice(u * 128, (u + 1) * 128)
        vec[0:8, cols] = jnp.where(lane < HEAD, blocks[2 * u], turned[2 * u + 1])[:8]
        vec[8:16, cols] = jnp.where(lane < HEAD, turned[2 * u], blocks[2 * u + 1])[:8]
    for t in range(16):
        for j in range(2):
            first = t * 256 + j * 128
            hidden_bias[:, first : first + 128] = blocks[t][7 + j : 8 + j]
    for u in range(4):
        row = blocks[4 * u]
        for j in range(1, 4):
            row = jnp.where(lane < 32 * j, row, pltpu.roll(blocks[4 * u + j], 32 * j, 1))
        down_bias[:, u * 128 : (u + 1) * 128] = row[9:10]


def attend_block(i, extent, causal, q_t, k, v_t, k_feat, q_feat, mix, mix_t, lse, even, odd, start, pairs):
    cols = pl.ds(i * QB if isinstance(i, int) else pl.multiple_of(i * QB, QB), QB)
    chunks = [(a, min(RB, extent - a)) for a in range(0, extent, RB)]
    empty = jnp.zeros((PAIR - 16, 2 * QB), BF16)

    def step(p, before, now):
        if before is not None:
            peak = jnp.full((8, 2 * QB), -3e38, F32)
            for a, w in chunks:
                peak = jnp.maximum(peak, jnp.max(before[a : a + w, :].reshape(w // 8, 8, 2 * QB), axis=0))
            peak = jnp.max(peak, axis=0, keepdims=True)
            total = jnp.zeros((8, 2 * QB), F32)
            acc = jnp.zeros((PAIR, 2 * QB), F32)
        if now is not None:
            wide = jnp.concatenate([two_heads(q_t[lanes_of(p + 1), cols]), twice(q_feat[:, cols]), empty], axis=0)
        for a, w in chunks:
            if now is not None:
                s = dot(jnp.concatenate([k[a : a + w, lanes_of(p + 1)], k_feat[a : a + w, :]], axis=1), wide)
                if causal and a + w == extent:
                    key = lax.broadcasted_iota(jnp.int32, (w, 2 * QB), 0) + a
                    query = lax.broadcasted_iota(jnp.int32, (w, 2 * QB), 1) % QB + i * QB
                    s = jnp.where(key <= query, s, -FAR)
                now[a : a + w, :] = s
            if before is not None:
                e = jnp.exp(before[a : a + w, :] - peak)
                total = total + jnp.sum(e.reshape(w // 8, 8, 2 * QB), axis=0)
                acc = acc + dot(v_t[lanes_of(p), a : a + w], e.astype(BF16))
        if before is not None:
            total = jnp.sum(total, axis=0, keepdims=True)
            out = one_of_each(acc * (1.0 / total)).astype(BF16)
            mix_t[lanes_of(p), cols] = out
            mix[cols, lanes_of(p)] = jnp.transpose(out)
            both = peak + jnp.log(total)
            lse[p, 0:1, cols] = both[:, :QB]
            lse[p, 1:2, cols] = both[:, QB:]

    def loop(g, _):
        step(start + 2 * g, even, odd)
        step(start + 2 * g + 1, odd, even)
        return 0

    step(start - 1, None, even)
    lax.fori_loop(0, pairs // 2 - 1, loop, 0)
    step(start + pairs - 2, even, odd)
    step(start + pairs - 1, odd, None)


SAVED = 16
(O_SQ, O_SK, O_SV, O_SM, O_CQ, O_CK, O_CV, O_CM, O_XH1, O_XH2, O_X2B, O_DH, O_DB, O_AB, O_R3, O_STAT) = range(SAVED)


def forward_kernel(remote, *refs):
    tokens, enc, dec_len, enc_len = refs[:4]
    arrays, refs = refs[4 : 5 + WEIGHTS], refs[5 + WEIGHTS :]
    gather = None
    if remote:
        extra = len(arrays) + 8
        gather = Gather(arrays, refs[: 1 + WEIGHTS], refs[-extra:-8], refs[-8:])
        arrays, refs = refs[: 1 + WEIGHTS], refs[1 + WEIGHTS : -extra]

    saved = refs[:SAVED]
    lse1, lse2, vec = refs[SAVED : SAVED + 3]
    (pool, even, odd, kf1, kf2, qf, xf, wslots, oslots, aslots, dbot, abot, stat, packed, hb, db, pool_s, w_s, out_s) = refs[SAVED + 3 :]
    X, ENC, QS, KS, VS, KC, VC, MIX, MTS, X1B, XH1, QC, MTC, X2B, XH2 = range(15)
    VTS, VTC = XH1, XH2
    DG = (X, ENC, KC, VC)
    n_rows = pool.shape[1] // RB

    loads = [pltpu.make_async_copy(tokens, pool.at[X], pool_s.at[0]), pltpu.make_async_copy(enc, pool.at[ENC], pool_s.at[1])]
    if gather is not None:
        for a in range(len(arrays)):
            gather.staged(a).start()
    for c in loads:
        c.start()
    if gather is not None:
        gather.barrier()
        gather.begin()

    free_slots = wslots.shape[0]
    fetches, slot_of = {}, {}
    for h in range(2):
        for k, w in enumerate(HALVED):
            at = slice(h * 512, (h + 1) * 512)
            fetches[w, h], slot_of[w, h] = (arrays[1 + w].at[:, :, :, at], wslots.at[k, :, :, :, at]), (0, k, h)
    for k, w in enumerate((CK, CV, SO, CQ, CO), 3):
        fetches[w], slot_of[w] = (arrays[1 + w], wslots.at[k % free_slots]), (0, k % free_slots, None)
    for k, w in enumerate((DOWN, UP)):
        fetches[w], slot_of[w] = (arrays[1 + w], aslots.at[k]), (1, k, None)
    for j in range(4):
        for h in range(2):
            if h == 0:
                fetches[HOUT, j] = (arrays[1 + HOUT].at[j], oslots.at[j % oslots.shape[0]])
                slot_of[HOUT, j] = (2, j % oslots.shape[0], None)
            at = slice(h * 512, (h + 1) * 512)
            source = arrays[1 + HIN].at[:, :, :, j * 1024 + h * 512 : j * 1024 + (h + 1) * 512]
            fetches[HIN, 2 * j + h] = (source, wslots.at[j % free_slots, :, :, :, at])
            slot_of[HIN, 2 * j + h] = (0, j % free_slots, h)
    order = list(fetches)

    def copy_of(k):
        return pltpu.make_async_copy(*fetches[k], w_s.at[order.index(k)])

    started, used = [], set()

    def arrived(k):
        return gather is None or gather.next[3] > piece_of(k)

    def piece_of(k):
        a, j = (k, None) if isinstance(k, int) else k
        found = [i for i, p in enumerate(gather.pieces) if p[0] == 1 + a]
        return found[-1] if j is None or a == HOUT else found[j]

    def ahead(k):
        kind, slot, half = slot_of[k]
        before = [u for u in order[: order.index(k)] if slot_of[u][:2] == (kind, slot)]
        return all(u in used for u in before if half is None or slot_of[u][2] in (None, half))

    def prefetch():
        while len(started) < len(order) and arrived(order[len(started)]) and ahead(order[len(started)]):
            copy_of(order[len(started)]).start()
            started.append(order[len(started)])

    def passed(us):
        if gather is not None:
            gather.passed(us)
        prefetch()

    def weight(k):
        if gather is not None:
            gather.until(piece_of(k))
        prefetch()
        assert k in started
        copy_of(k).wait()
        ref = fetches[k][1]
        return lambda: ref[...].reshape(-1, ref.shape[-1])

    writes = []

    def write(src, slot, dst=None):
        c = pltpu.make_async_copy(src, saved[slot] if dst is None else dst, out_s.at[len(writes)])
        c.start()
        writes.append(c)

    dec_ends, enc_ends = ends_of(dec_len), ends_of(enc_len)
    key_features(kf1, dec_ends)
    key_features(kf2, enc_ends)
    qf[...] = query_features(0, qf.shape[1], dec_ends).astype(BF16)
    if gather is not None:
        gather.whole(VEC)
    packed_in = pltpu.make_async_copy(arrays[VEC], packed, pool_s.at[2])
    packed_in.start()
    packed_in.wait()
    unpack_vectors([packed[t // NB, t % NB] for t in range(NZ * NB)], vec, hb, db)
    for c in loads:
        c.wait()

    def project(src, w, dst, b=None, factor=None, turned=None, at=slice(0, 1024)):
        get = weight(w)

        def block(i, _):
            r = dot(pool[src, rows_of(i), :], get())
            if b is not None:
                r = r + vec[b : b + 1, at]
            r = r.astype(BF16)
            if factor is not None:
                r = r * jnp.asarray(factor, BF16)
            if dst is not None:
                pool[dst, rows_of(i), at] = r
            if turned is not None:
                pool[turned, at, rows_of(i)] = jnp.transpose(r)
            return 0

        lax.fori_loop(0, n_rows, block, 0)
        used.add(w)
        passed(3 * (at.stop - at.start) / 1024)

    shrink = HEAD ** (-0.5)
    n_blocks = pool.shape[1] // QB
    for h in range(2):
        at = slice(h * 512, (h + 1) * 512)
        project(X, (SQ, h), None, SQB, shrink, QS, at)
        project(X, (SK, h), KS, at=at)
        project(X, (SV, h), VS, SVB, None, VTS, at)
        if h == 1:
            write(pool.at[QS], O_SQ)
            write(pool.at[KS], O_SK)
            write(pool.at[VS], O_SV)
        for i in range(n_blocks):
            attend_block(i, (i + 1) * QB, True, pool.at[QS], pool.at[KS], pool.at[VTS], kf1, qf, pool.at[MIX], pool.at[MTS], lse1, even, odd, 4 * h, 4)
            passed(0.33 * (i + 1))
    write(pool.at[MTS], O_SM)
    project(ENC, CK, KC)
    project(ENC, CV, VC, CVB, None, VTC)
    write(pool.at[KC], O_CK)
    write(pool.at[VC], O_CV)

    def mix_out(mixed, w, b, residual, gain, shift, low_slot, hat_slot, column):
        get = weight(w)

        def block(i, _):
            r = residual(i) + dot(pool[mixed, rows_of(i), :], get()) + vec[b : b + 1, :]
            xhat, rstd = normalized(r)
            y = xhat * vec[gain : gain + 1, :] + vec[shift : shift + 1, :]
            xf[rows_of(i), :] = y
            pool[low_slot, rows_of(i), :] = y.astype(BF16)
            pool[hat_slot, rows_of(i), :] = xhat.astype(BF16)
            stat[column, rows_of(i), :] = jnp.broadcast_to(rstd, (RB, 128))
            return 0

        lax.fori_loop(0, n_rows, block, 0)
        used.add(w)
        passed(4)

    mix_out(MIX, SO, SOB, lambda i: pool[X, rows_of(i), :].astype(F32), G1, S1, X1B, XH1, 0)
    write(pool.at[XH1], O_XH1)
    project(X1B, CQ, None, CQB, shrink, QC)
    write(pool.at[QC], O_CQ)
    for part in range(4):

        def block(i, _):
            attend_block(i, pool.shape[1], False, pool.at[QC], pool.at[KC], pool.at[VTC], kf2, qf, pool.at[MIX], pool.at[MTC], lse2, even, odd, 0, 8)
            return 0

        lax.fori_loop(part * n_blocks // 4, (part + 1) * n_blocks // 4, block, 0)
        passed(8)
    write(pool.at[MTC], O_CM)
    mix_out(MIX, CO, COB, lambda i: xf[rows_of(i), :], G2, S2, X2B, XH2, 1)
    write(pool.at[XH2], O_XH2)
    write(pool.at[X2B], O_X2B)
    write(stat, O_STAT)

    down, up = weight(DOWN), weight(UP)

    def adapter(i, _):
        pre = dot_nt(pool[X2B, rows_of(i), :], down()) + db[...]
        act, slope = gelu_parts(pre)
        low = act.astype(BF16)
        abot[rows_of(i), :] = low
        dbot[rows_of(i), :] = slope.astype(BF16)
        more = dot(low, up()) + vec[AUB : AUB + 1, :]
        xf[rows_of(i), :] = xf[rows_of(i), :] + vec[HOB : HOB + 1, :] + SCALE * more
        return 0

    lax.fori_loop(0, n_rows, adapter, 0)
    passed(5)
    write(abot, O_AB)
    write(dbot, O_DB)
    for c in writes[:7]:
        c.wait()
    for j in range(8):
        if j % 2 == 0:
            w_out = weight((HOUT, j // 2))
        w_in = weight((HIN, j))
        at, rows_at = slice(j * 512, (j + 1) * 512), slice(j % 2 * 512, j % 2 * 512 + 512)

        def into(i, w_in=w_in, at=at):
            return dot(pool[X2B, rows_of(i), :], w_in()) + hb[:, at]

        def out_of(i, pre, j=j, w_out=w_out, rows_at=rows_at):
            act, slope = gelu_parts(pre)
            pool[DG[j // 2], rows_of(i), rows_at] = slope.astype(BF16)
            xf[rows_of(i), :] = xf[rows_of(i), :] + dot(act.astype(BF16), w_out()[rows_at, :])

        def hidden(g, _):
            first, second = into(2 * g), into(2 * g + 1)
            out_of(2 * g, first)
            out_of(2 * g + 1, second)
            return 0

        lax.fori_loop(0, n_rows // 2, hidden, 0)
        used.add((HIN, j))
        if j % 2:
            used.add((HOUT, j // 2))
        passed(4.5)
        if j % 2:
            half = j // 2
            write(pool.at[DG[half]], O_DH, saved[O_DH].at[:, half * 1024 : (half + 1) * 1024])
    write(xf, O_R3)
    for c in writes[7:]:
        c.wait()
    if gather is not None:
        gather.finish()


def forward(tokens, enc, dec_len, enc_len, arrays, remote):
    slots, width = tokens.shape
    hidden = arrays[1 + HIN].shape[-1]
    bottle = arrays[1 + DOWN].size // width * (NZ * NB if remote else 1)
    bf, f3 = functools.partial(jax.ShapeDtypeStruct, dtype=BF16), functools.partial(jax.ShapeDtypeStruct, dtype=F32)
    main = bf((slots, width))
    outs = [main] * 11 + [bf((slots, hidden)), bf((slots, bottle)), bf((slots, bottle)), f3((slots, width)), f3((2, slots, 128))]
    outs += [f3((width // PAIR, 2, slots)), f3((width // PAIR, 2, slots)), f3((16, width))]
    gathered = [bf((NZ, NB) + a.shape) for a in arrays] if remote else []
    params = dict(collective_id=0, has_side_effects=True) if remote else {}
    kept = pl.pallas_call(
        functools.partial(forward_kernel, remote),
        out_shape=gathered + outs,
        in_specs=[ANY, ANY, SMEM, SMEM] + [ANY] * len(arrays),
        out_specs=[ANY] * (len(gathered) + SAVED) + [WHOLE] * 3,
        scratch_shapes=[
            pltpu.VMEM((15, slots, width), BF16),
            pltpu.VMEM((slots, 2 * QB), F32),
            pltpu.VMEM((slots, 2 * QB), F32),
            pltpu.VMEM((slots, PAIR), BF16),
            pltpu.VMEM((slots, PAIR), BF16),
            pltpu.VMEM((16, slots), BF16),
            pltpu.VMEM((slots, width), F32),
            pltpu.VMEM((4, NZ, NB, 64, 1024), BF16),
            pltpu.VMEM((2, NB, 256, 1024), BF16),
            pltpu.VMEM((2, NZ, NB, bottle // 16, 1024), BF16),
            pltpu.VMEM((slots, bottle), BF16),
            pltpu.VMEM((slots, bottle), BF16),
            pltpu.VMEM((2, slots, 128), F32),
            pltpu.VMEM((NZ, NB, 32, 128), BF16),
            pltpu.VMEM((1, hidden), F32),
            pltpu.VMEM((1, bottle), F32),
            pltpu.SemaphoreType.DMA((3,)),
            pltpu.SemaphoreType.DMA((32,)),
            pltpu.SemaphoreType.DMA((24,)),
        ] + (gather_scratch([a.shape for a in arrays]) if remote else []),
        compiler_params=pltpu.CompilerParams(vmem_limit_bytes=VMEM, **params),
        cost_estimate=cost(slots * (16 * width * width + 4 * slots * width * 8), *arrays, *outs),
        name="forward",
    )(tokens, enc, dec_len, enc_len, *arrays)
    return (kept[: len(gathered)] or list(arrays)), kept[len(gathered) :]


def head_sums(grad_t, mix_t):
    product = grad_t.astype(F32) * mix_t.astype(F32)
    return jnp.sum(product.reshape(-1, HEAD, product.shape[1]), axis=1)


def head_back_kernel(dec_len, r3, cot, vec, db, ab, x2b, down, up, out, g3, g3b, grads, gbias):
    i = pl.program_id(0)
    ends = ends_of(dec_len)
    xhat, rstd = normalized(r3[...])
    gain = vec[G3 : G3 + 1, :]
    out[...] = (xhat * gain + vec[S3 : S3 + 1, :]).astype(BF16)
    pos = lax.broadcasted_iota(jnp.int32, r3.shape, 0) + i * r3.shape[0]
    upstream = jnp.where(pos < ends[2], cot[...].astype(F32), 0.0)
    g = norm_back(xhat, rstd, gain, upstream)
    g3b[...] = g.astype(BF16)
    g_adapt = (SCALE * g).astype(BF16)
    g_bottle = (db[...].astype(F32) * dot_nt(g_adapt, up[...])).astype(BF16)
    g3[...] = g + dot(g_bottle, down[...])

    @pl.when(i == 0)
    def _():
        grads[...] = jnp.zeros_like(grads)
        gbias[...] = jnp.zeros_like(gbias)

    grads[0] = grads[0] + dot_tn(g_bottle, x2b[...])
    grads[1] = grads[1] + dot_tn(ab[...], g_adapt)
    gbias[0:1, :] = gbias[0:1, :] + jnp.sum(g_adapt.astype(F32), axis=0, keepdims=True)
    wide = gbias[1:2, 0 : db.shape[1]]
    gbias[1:2, 0 : db.shape[1]] = wide + jnp.sum(g_bottle.astype(F32), axis=0, keepdims=True)


def full(shape):
    return pl.BlockSpec(shape, lambda *_: (0,) * len(shape))


def head_back(dec_len, r3, cot, vec, db, ab, x2b, down, up):
    slots, width = r3.shape
    bottle = db.shape[1]
    sds = jax.ShapeDtypeStruct
    row, low = pl.BlockSpec((RB, width), lambda i: (i, 0)), pl.BlockSpec((RB, bottle), lambda i: (i, 0))
    outs = [
        sds((slots, width), BF16), sds((slots, width), F32), sds((slots, width), BF16),
        sds((2, bottle, width), F32), sds((8, width), F32),
    ]
    return pl.pallas_call(
        head_back_kernel,
        grid=(slots // RB,),
        out_shape=outs,
        in_specs=[SMEM, row, row, full(vec.shape), low, low, row, full(down.shape), full(up.shape)],
        out_specs=[row] * 3 + [full(o.shape) for o in outs[3:]],
        compiler_params=pltpu.CompilerParams(vmem_limit_bytes=VMEM),
        cost_estimate=cost(slots * 4 * width * bottle, *outs, r3, cot),
        name="head_back",
    )(dec_len, r3, cot, vec, db, ab, x2b, down, up)


class Reduce:
    def __init__(self, grads, gbias, shares, bias, scratch):
        self.grads, self.gbias, self.shares, self.bias = grads, gbias, shares, bias
        (self.s1, self.r1, self.s2, self.r2, self.s3, self.r3, self.s4, self.r4, self.f5, self.r5,
         self.sb, self.rb, self.acc2, self.acc3, self.send, self.recv) = scratch
        self.core, t = lax.axis_index("grp"), lax.axis_index("tok")
        self.z, b = t // NB, t % NB
        self.y, self.x = b // 2, b % 2
        self.b = b
        by_x, by_y = self.y * 2 + (1 - self.x), (1 - self.y) * 2 + self.x
        core, z = self.core, self.z
        n2, n3 = by_x + core * (by_y - by_x), by_y + core * (by_x - by_y)
        self.across = {"grp": 1 - core, "tok": t}
        self.second = {"grp": core, "tok": z * NB + n2}
        self.third = {"grp": core, "tok": z * NB + n3}
        self.along = [{"grp": core, "tok": (z + d) % NZ * NB + b} for d in (1, 2, 3)]

    def copy(self, n, src, dst, to):
        return pltpu.make_async_remote_copy(src, dst, self.send.at[n], self.recv.at[n], device_id=to, device_id_type=MESH)

    def copies(self, stage):
        if stage == 1:
            return [self.copy(0, self.s1, self.r1, self.across), self.copy(1, self.sb.at[0], self.rb.at[0], self.across)]
        if stage == 2:
            return [self.copy(2, self.s2, self.r2, self.second), self.copy(3, self.sb.at[1], self.rb.at[1], self.second)]
        if stage == 3:
            return [self.copy(4, self.s3, self.r3, self.third), self.copy(5, self.sb.at[2], self.rb.at[2], self.third)]
        if stage == 4:
            moves = [self.copy(6 + d, self.s4.at[d], self.r4.at[d], self.along[d]) for d in range(3)]
            return moves + [self.copy(9 + d, self.sb.at[3], self.rb.at[3 + d], self.along[d]) for d in range(3)]
        return [self.copy(12, self.f5, self.r5, self.across)]

    def go(self, stage):
        for c in self.copies(stage):
            c.start()

    def wait(self, stage):
        for c in self.copies(stage):
            c.wait()

    def begin(self):
        sem = pltpu.get_barrier_semaphore()
        for peer in [self.across, self.second, self.third, *self.along]:
            pl.semaphore_signal(sem, inc=1, device_id=peer, device_id_type=MESH)
        pl.semaphore_wait(sem, 6)
        self.s1[...] = self.grads[1 - self.core].astype(BF16)
        self.bias[...] = jnp.concatenate([self.gbias[...], jnp.zeros_like(self.gbias[...])], axis=0)
        self.sb[0] = self.bias[...].astype(BF16)
        self.go(1)

    def add_bias(self, n, more):
        self.bias[...] = self.bias[...] + more
        self.sb[n] = self.bias[...].astype(BF16)

    def first(self):
        self.wait(1)
        total = self.grads[self.core] + self.r1[...].astype(F32)
        rows, width = total.shape[0] // (NZ * NB), total.shape[1]
        total = total.reshape(NZ, 2, 2, rows, width)
        by_x = [total[:, :, k].reshape(2 * NZ, rows, width) for k in range(2)]
        by_y = [total[:, k].reshape(2 * NZ, rows, width) for k in range(2)]
        even, odd = [jnp.where(self.core == 0, u, v) for u, v in zip(by_x, by_y)]
        high = jnp.where(self.core == 0, self.x, self.y) == 1
        self.acc2[...] = jnp.where(high, odd, even)
        self.s2[...] = jnp.where(high, even, odd).astype(BF16)
        self.add_bias(1, self.rb[0].astype(F32))
        self.go(2)

    def next(self):
        self.wait(2)
        total = self.acc2[...] + self.r2[...].astype(F32)
        total = total.reshape((NZ, 2) + total.shape[1:])
        high = jnp.where(self.core == 0, self.y, self.x) == 1
        self.acc3[...] = jnp.where(high, total[:, 1], total[:, 0])
        self.s3[...] = jnp.where(high, total[:, 0], total[:, 1]).astype(BF16)
        self.add_bias(2, self.rb[1].astype(F32))
        self.go(3)

    def then(self):
        self.wait(3)
        self.acc3[...] = self.acc3[...] + self.r3[...].astype(F32)
        for d in range(3):
            self.s4[d] = self.acc3[(self.z + d + 1) % NZ].astype(BF16)
        self.add_bias(3, self.rb[2].astype(F32))
        self.go(4)

    def last(self):
        self.wait(4)
        total = self.acc3[self.z]
        for d in range(3):
            total = total + self.r4[d].astype(F32)
        self.bias[...] = self.bias[...] + self.rb[3].astype(F32) + self.rb[4].astype(F32) + self.rb[5].astype(F32)
        self.f5[...] = total
        self.shares[self.core] = total
        self.go(5)

    def end(self):
        self.wait(5)
        self.shares[1 - self.core] = self.r5[...]


def reduce_scratch(bottle, width):
    vmem, rows = pltpu.VMEM, bottle // (NZ * NB)
    pairs = [(NZ * NB,), (2 * NZ,), (NZ,), (3,)]
    bufs = [vmem((bottle, width), BF16)] * 2
    for lead in pairs[1:]:
        bufs += [vmem(lead + (rows, width), BF16)] * 2
    bufs += [vmem((rows, width), F32)] * 2
    bufs += [vmem((4, 16, width), BF16), vmem((6, 16, width), BF16)]
    bufs += [vmem((2 * NZ, rows, width), F32), vmem((NZ, rows, width), F32)]
    return bufs + [pltpu.SemaphoreType.DMA((13,))] * 2


def ffn_back_kernel(remote, vec, g3b, dh, w_out, w_in, grads, gbias, g3, xh2, stat, cm, co, gr2, gmix, delta, shares, bias,
                    acc, g3_v, xh2_v, stat_v, cm_v, co_v, sems, *scratch):
    step = pl.program_id(0)
    n_rows = g3b.shape[0] // RB
    if remote:
        reduce = Reduce(grads, gbias, shares, bias, scratch)
        for n, part in enumerate((reduce.begin, reduce.first, reduce.next, reduce.then)):
            pl.when(step == n)(part)
    moves = [(g3, g3_v), (xh2, xh2_v), (stat, stat_v), (cm, cm_v), (co, co_v)]
    copies = [pltpu.make_async_copy(a, b, sems.at[n]) for n, (a, b) in enumerate(moves)]

    @pl.when(step == 0)
    def _():
        for c in copies:
            c.start()
        acc[...] = jnp.zeros_like(acc)

    def hidden(i, _):
        blocks = [rows_of(2 * i), rows_of(2 * i + 1)]
        pres = [dot_nt(g3b[rows, :], w_out[...]) for rows in blocks]
        for rows, pre in zip(blocks, pres):
            g = (dh[rows, :].astype(F32) * pre).astype(BF16)
            acc[rows, :] = acc[rows, :] + dot_nt(g, w_in[...])
        return 0

    lax.fori_loop(0, n_rows // 2, hidden, 0)

    @pl.when(step == pl.num_programs(0) - 1)
    def _():
        if remote:
            reduce.last()
        for c in copies:
            c.wait()

        def last(i, _):
            rows = rows_of(i)
            g = acc[rows, :] + g3_v[rows, :]
            g = norm_back(xh2_v[rows, :].astype(F32), stat_v[1, rows, 0:1], vec[G2 : G2 + 1, :], g)
            gr2[rows, :] = g
            mix = dot_nt(co_v[...], g.astype(BF16)).astype(BF16)
            gmix[:, rows] = mix
            delta[:, rows] = head_sums(mix, cm_v[:, rows])
            return 0

        lax.fori_loop(0, n_rows, last, 0)
        if remote:
            reduce.end()


def ffn_back(remote, vec, g3b, dh, w_out, w_in, grads, gbias, g3, xh2, stat, cm, co):
    slots, width = g3.shape
    hidden = dh.shape[1]
    step = 1024
    sds = jax.ShapeDtypeStruct
    bottle = grads.shape[1]
    outs = [sds((slots, width), F32), sds((width, slots), BF16), sds((width // HEAD, slots), F32)]
    outs += [sds((2, bottle // (NZ * NB), width), F32), sds((16, width), F32)]
    late = [g3, xh2, stat, cm, co]
    params = dict(collective_id=1, has_side_effects=True) if remote else {}
    return pl.pallas_call(
        functools.partial(ffn_back_kernel, remote),
        grid=(hidden // step,),
        out_shape=outs,
        in_specs=[
            full(vec.shape), full(g3b.shape),
            pl.BlockSpec((slots, step), lambda c: (0, c)),
            pl.BlockSpec((step, width), lambda c: (c, 0)),
            pl.BlockSpec((width, step), lambda c: (0, c)),
            full(grads.shape), full(gbias.shape),
        ] + [ANY] * len(late),
        out_specs=[full(o.shape) for o in outs],
        scratch_shapes=[pltpu.VMEM((slots, width), F32)]
        + [pltpu.VMEM(a.shape, a.dtype) for a in late]
        + [pltpu.SemaphoreType.DMA((len(late),))]
        + (reduce_scratch(bottle, width) if remote else []),
        compiler_params=pltpu.CompilerParams(vmem_limit_bytes=VMEM, **params),
        cost_estimate=cost(slots * width * (2 * hidden + width), *outs, dh, w_out, w_in, co),
        name="ffn_back",
    )(vec, g3b, dh, w_out, w_in, grads, gbias, *late)


def cross_tail(i, dq, dk, dv, vec, gr2, xh1, stat, sm, cq, ck, cv, so, genc, gmix, delta):
    rows = rows_of(i)
    genc[rows, :] = (dot_nt(dk[rows, :], ck[...]) + dot_nt(dv[rows, :], cv[...])).astype(BF16)
    g = gr2[rows, :] + dot_nt(dq[rows, :], cq[...])
    g = norm_back(xh1[rows, :].astype(F32), stat[0, rows, 0:1], vec[G1 : G1 + 1, :], g)
    gr2[rows, :] = g
    mix = dot_nt(so[...], g.astype(BF16)).astype(BF16)
    gmix[:, rows] = mix
    delta[:, rows] = head_sums(mix, sm[:, rows])


def self_tail(i, dq, dk, dv, gr1, sq, sk, sv, gtok):
    rows = rows_of(i)
    g = gr1[rows, :] + dot_nt(dq[rows, :], sq[...]) + dot_nt(dk[rows, :], sk[...]) + dot_nt(dv[rows, :], sv[...])
    gtok[rows, :] = g.astype(BF16)


def attend_back_kernel(causal, q_len, k_len, q_t, k, v, g_t, lse, delta, *rest):
    if causal:
        late, outs, rest = rest[:4], rest[4:5], rest[5:]
        late_v, staged, rest = rest[:4], rest[4:5], rest[5:]
    else:
        vec, late, outs, new_delta, rest = rest[0], rest[1:9], rest[9:12], rest[12], rest[13:]
        late_v, staged, rest = rest[:8], rest[8:10], rest[10:]
    (dq, dk, dv, late_s, out_s, dk_t, dv_t, dq_t, k_t, qx, gx, kf, s_buf, d_buf, tile_i, tile_j, new_q, new_k, tiles) = rest
    step = pl.program_id(0)

    @pl.when(step == 0)
    def _():
        for n, (src, dst) in enumerate(zip(late, late_v)):
            pltpu.make_async_copy(src, dst, late_s.at[n]).start()

    slots, pairs = k.shape[0], k.shape[1] // PAIR
    blocks = slots // QB
    q_ends, k_ends = ends_of(q_len), ends_of(k_len)

    @pl.when(pl.program_id(0) == 0)
    def _():
        key_features(kf, k_ends)
        count = jnp.int32(0)
        reached = jnp.int32(0)
        for i in range(blocks):
            low, _ = pick(segment(jnp.int32(i * QB), q_ends), k_ends, 0, slots)
            _, high = pick(segment(jnp.int32(i * QB + QB - 1), q_ends), k_ends, 0, slots)
            if causal:
                high = jnp.minimum(high, (i + 1) * QB)

            def put(j, n, i=i, low=low, reached=reached):
                tile_i[n] = i
                tile_j[n] = j
                new_q[n] = (j == low // KB).astype(jnp.int32)
                new_k[n] = (j >= reached).astype(jnp.int32)
                return n + 1

            count = lax.fori_loop(low // KB, (high + KB - 1) // KB, put, count)
            reached = jnp.maximum(reached, (high + KB - 1) // KB)
        tiles[0] = count

    k_t[...] = jnp.transpose(k[...])
    empty = jnp.zeros((PAIR - 16, 2 * QB), BF16)
    for i in range(blocks):
        cols = slice(i * QB, (i + 1) * QB)
        far = twice(query_features(i * QB, QB, q_ends))
        for n in range(pairs):
            part = slice(n * PAIR, (n + 1) * PAIR)
            both_lse = jnp.concatenate([lse[n, 0:1, cols], lse[n, 1:2, cols]], axis=1)
            both_delta = jnp.concatenate([delta[2 * n : 2 * n + 1, cols], delta[2 * n + 1 : 2 * n + 2, cols]], axis=1)
            qx[n, i, :PAIR, :] = two_heads(q_t[part, cols])
            qx[n, i, PAIR : PAIR + 16, :] = (far + in_parts(-both_lse, 4)).astype(BF16)
            qx[n, i, PAIR + 16 :, :] = empty
            gx[n, i, :PAIR, :] = two_heads(g_t[part, cols])
            gx[n, i, PAIR : PAIR + 16, :] = in_parts(-both_delta, 4).astype(BF16)
            gx[n, i, PAIR + 16 :, :] = empty

    if causal:
        shape = (KB, 2 * QB)
        ahead = lax.broadcasted_iota(jnp.int32, shape, 0) - lax.broadcasted_iota(jnp.int32, shape, 1) % QB

    def keys_of(j):
        return pl.ds(pl.multiple_of(j * KB, KB), KB)

    def scores(t, n):
        i, keys = tile_i[t], keys_of(tile_j[t])
        part = slice(n * PAIR, (n + 1) * PAIR)
        s_buf[n] = dot(jnp.concatenate([k[keys, part], kf[keys, :]], axis=1), qx[n, i])
        d_buf[n] = dot(jnp.concatenate([v[keys, part], kf[keys, :]], axis=1), gx[n, i])

    def grads(t, n):
        i, j = tile_i[t], tile_j[t]
        keys = keys_of(j)
        p = jnp.exp(s_buf[n])
        if causal:
            p = jnp.where(ahead <= i * QB - j * KB, p, 0.0)
        d = (p * d_buf[n]).astype(BF16)
        first_q, first_k = new_q[t] == 1, new_k[t] == 1
        dv_t[n, :, keys] = jnp.where(first_k, 0.0, dv_t[n, :, keys]) + dot_nt(gx[n, i, :PAIR, :], p.astype(BF16))
        dk_t[n, :, keys] = jnp.where(first_k, 0.0, dk_t[n, :, keys]) + dot_nt(qx[n, i, :PAIR, :], d)
        dq_t[n, i] = jnp.where(first_q, 0.0, dq_t[n, i]) + dot(k_t[n * PAIR : (n + 1) * PAIR, keys], d)

    def loop(t, _):
        for n in range(pairs):
            grads(t - 1, n)
            scores(t, n)
        return 0

    last = tiles[0]
    for n in range(pairs):
        scores(0, n)
    lax.fori_loop(1, last, loop, 0)
    for n in range(pairs):
        grads(last - 1, n)
    for n in range(pairs):
        part = pl.ds(pl.multiple_of((step * pairs + n) * PAIR, PAIR), PAIR)
        dk[:, part] = jnp.transpose(dk_t[n].astype(BF16))
        dv[:, part] = jnp.transpose(dv_t[n].astype(BF16))
        for i in range(blocks):
            dq[i * QB : (i + 1) * QB, part] = jnp.transpose((one_of_each(dq_t[n, i]) * HEAD ** (-0.5)).astype(BF16))

    @pl.when(step == pl.num_programs(0) - 1)
    def _():
        for n, (src, dst) in enumerate(zip(late, late_v)):
            pltpu.make_async_copy(src, dst, late_s.at[n]).wait()
        results = [*staged] if causal else [staged[0], late_v[0], staged[1]]

        def back(n, i):
            at = (slice(None), rows_of(i)) if n == 2 else (rows_of(i), slice(None))
            return pltpu.make_async_copy(results[n].at[at], outs[n].at[at], out_s.at[n, i])

        def tail(i, _):
            if causal:
                self_tail(i, dq, dk, dv, *late_v, staged[0])
            else:
                cross_tail(i, dq, dk, dv, vec, *late_v, *staged, new_delta)
            for n in range(len(outs)):
                back(n, i).start()
            return 0

        lax.fori_loop(0, slots // RB, tail, 0)
        for i in range(slots // RB):
            for n in range(len(outs)):
                back(n, i).wait()


def attend_back(causal, q_len, k_len, q_t, k, v, g_t, lse, delta, vec, late, group=4):
    slots, width = k.shape
    pairs, blocks, heads = width // PAIR, slots // QB, width // HEAD
    col = pl.BlockSpec((slots, group * PAIR), lambda p: (0, p))
    row = pl.BlockSpec((group * PAIR, slots), lambda p: (p, 0))
    stat = pl.BlockSpec((group, 2, slots), lambda p: (p, 0, 0))
    vmem, sds = pltpu.VMEM, jax.ShapeDtypeStruct
    outs, specs, staged = [sds((slots, width), BF16)], [ANY], [vmem((slots, width), BF16)]
    extra, extra_specs = [], []
    if not causal:
        outs += [sds((slots, width), F32), sds((width, slots), BF16), sds((heads, slots), F32)]
        specs += [ANY, ANY, full((heads, slots))]
        staged += [vmem((width, slots), BF16)]
        extra, extra_specs = [vec], [full(vec.shape)]
    return pl.pallas_call(
        functools.partial(attend_back_kernel, causal),
        grid=(pairs // group,),
        out_shape=outs,
        in_specs=[SMEM, SMEM, row, col, col, row, stat, pl.BlockSpec((2 * group, slots), lambda p: (p, 0))]
        + extra_specs + [ANY] * len(late),
        out_specs=specs,
        scratch_shapes=[vmem(a.shape, a.dtype) for a in late] + staged + [
            vmem((slots, width), BF16),
            vmem((slots, width), BF16),
            vmem((slots, width), BF16),
            pltpu.SemaphoreType.DMA((len(late),)),
            pltpu.SemaphoreType.DMA((3, slots // RB)),
            vmem((group, PAIR, slots), F32),
            vmem((group, PAIR, slots), F32),
            vmem((group, blocks, PAIR, 2 * QB), F32),
            vmem((group * PAIR, slots), BF16),
            vmem((group, blocks, 2 * PAIR, 2 * QB), BF16),
            vmem((group, blocks, 2 * PAIR, 2 * QB), BF16),
            vmem((slots, PAIR), BF16),
            vmem((group, KB, 2 * QB), F32),
            vmem((group, KB, 2 * QB), F32),
            pltpu.SMEM((blocks * blocks,), jnp.int32),
            pltpu.SMEM((blocks * blocks,), jnp.int32),
            pltpu.SMEM((blocks * blocks,), jnp.int32),
            pltpu.SMEM((blocks * blocks,), jnp.int32),
            pltpu.SMEM((1,), jnp.int32),
        ],
        compiler_params=pltpu.CompilerParams(vmem_limit_bytes=VMEM),
        cost_estimate=cost(5 * slots * slots * width * 4 + 4 * slots * width * width, k, v, k, v, *late),
        name="self_back" if causal else "cross_back",
    )(q_len, k_len, q_t, k, v, g_t, lse, delta, *extra, *late)


def local(groups, tokens, enc, dec_len, enc_len, cot, sq, sqb, sk, sv, svb, so, sob, g1, s1, cq, cqb, ck, cv, cvb, co, cob,
          g2, s2, hin, hinb, hout, houtb, g3, s3, down, downb, up, upb):
    vectors = (sqb, svb, sob, g1, s1, cqb, cvb, cob, g2, s2, houtb, g3, s3, upb)
    weights = (sq, sk, sv, ck, cv, so, cq, co, down, up, hout, hin)
    remote = groups == NZ * NB
    if remote:
        arrays = [pack_vectors(vectors, hinb, downb, 1)[0], *weights]
    else:
        every = functools.partial(lax.all_gather, axis_name="tok", axis=0, tiled=True)
        packed = pack_vectors([every(v) for v in vectors], every(hinb), every(downb), NZ * NB)
        arrays = [packed.reshape(NZ, NB, 32, 128)]
        arrays += [every(w).reshape(NZ, NB, w.shape[0] * groups // (NZ * NB), w.shape[1]) for w in weights]
    arrays, kept = forward(tokens, enc, dec_len, enc_len, arrays, remote)
    flat = [a.reshape(-1, a.shape[-1]) for a in arrays[1:]]
    lse1, lse2, vec = kept[SAVED:]
    out, g3, g3b, grads, gbias = head_back(
        dec_len, kept[O_R3], cot, vec, kept[O_DB], kept[O_AB], kept[O_X2B], flat[DOWN], flat[UP]
    )
    _, bottle, width = grads.shape
    if not remote:
        parts = [grads[0].reshape(groups, -1, width), grads[1].reshape(groups, -1, width), jnp.broadcast_to(gbias[None], (groups, 8, width))]
        share = lax.psum_scatter(jnp.concatenate(parts, axis=1).astype(BF16), "tok", scatter_dimension=0, tiled=False)
    gr2, gmix, delta, shares, bias = ffn_back(
        remote, vec, g3b, kept[O_DH], flat[HOUT], flat[HIN], grads, gbias, g3, kept[O_XH2], kept[O_STAT], kept[O_CM], flat[CO]
    )
    genc, gr1, gmix, delta = attend_back(
        False, dec_len, enc_len, kept[O_CQ], kept[O_CK], kept[O_CV], gmix, lse2, delta, vec,
        (gr2, kept[O_XH1], kept[O_STAT], kept[O_SM], flat[CQ], flat[CK], flat[CV], flat[SO]),
    )
    (gtok,) = attend_back(
        True, dec_len, dec_len, kept[O_SQ], kept[O_SK], kept[O_SV], gmix, lse1, delta, vec,
        (gr1, flat[SQ], flat[SK], flat[SV]),
    )
    rows = bottle // groups
    if not remote:
        total = lax.psum(share, "grp").astype(F32)
        shares, bias = total[: 2 * rows].reshape(2, rows, width), total[2 * rows :]
    me = lax.axis_index("tok")
    up_bias = lax.dynamic_slice(bias[0], (me * (width // groups),), (width // groups,))
    down_bias = lax.dynamic_slice(bias[1], (me * rows,), (rows,))
    return out, gtok, genc, shares[0], down_bias, shares[1], up_bias


def solution(mesh):
    split = P(("grp", "tok"), None)
    two, one = P("tok", None), P("tok")
    ranks = [2, 1, 2, 2, 1, 2, 1, 1, 1, 2, 1, 2, 2, 1, 2, 1, 1, 1, 2, 1, 2, 1, 1, 1, 2, 1, 2, 1]
    return jax.shard_map(
        functools.partial(local, mesh.shape["tok"]),
        mesh=mesh,
        in_specs=(split,) * 5 + tuple(two if r == 2 else one for r in ranks),
        out_specs=(split,) * 3 + (two, one, two, one),
        check_vma=False,
    )
```

```python
import functools

import jax
import jax.numpy as jnp
from jax import lax
from jax.experimental import pallas as pl
from jax.experimental.pallas import tpu as pltpu
from jax.sharding import PartitionSpec as P

F32 = jnp.float32
BF16 = jnp.bfloat16
HEAD = 64
PAIR = 2 * HEAD
EPSILON = 1e-05
SCALE = 4.0
RB = 256
QB = 128
KB = 256
FAR = float(1 << 30)
MIB = 1 << 20
VMEM = 62 * MIB
MESH = pl.DeviceIdType.MESH
ANY = pl.BlockSpec(memory_space=pl.ANY)
SMEM = pl.BlockSpec(memory_space=pltpu.SMEM)
WHOLE = pl.BlockSpec(memory_space=pltpu.VMEM)


def dot(a, b):
    return jnp.dot(a, b, preferred_element_type=F32)


def dot_nt(a, b):
    return lax.dot_general(a, b, (((1,), (1,)), ((), ())), preferred_element_type=F32)


def dot_tn(a, b):
    return lax.dot_general(a, b, (((0,), (0,)), ((), ())), preferred_element_type=F32)


def cost(macs, *arrays):
    return pl.CostEstimate(flops=2 * macs, bytes_accessed=sum(a.size * a.dtype.itemsize for a in arrays), transcendentals=0)


def rows_of(i):
    return pl.ds(pl.multiple_of(i * RB, RB), RB)


def lanes_of(p):
    return pl.ds(pl.multiple_of(p * PAIR, PAIR), PAIR)


def two_heads(values):
    row = lax.broadcasted_iota(jnp.int32, values.shape, 0)
    zero = jnp.zeros_like(values)
    return jnp.concatenate([jnp.where(row < HEAD, values, zero), jnp.where(row < HEAD, zero, values)], axis=1)


def one_of_each(values):
    n = values.shape[1] // 2
    row = lax.broadcasted_iota(jnp.int32, (values.shape[0], n), 0)
    return jnp.where(row < HEAD, values[:, :n], values[:, n:])


def twice(values):
    return jnp.concatenate([values, values], axis=1)


def normalized(r):
    centred = r - jnp.mean(r, axis=-1, keepdims=True)
    rstd = lax.rsqrt(jnp.mean(centred * centred, axis=-1, keepdims=True) + EPSILON)
    return centred * rstd, rstd


def norm_back(xhat, rstd, gain, upstream):
    u = upstream * gain
    first = jnp.mean(u, axis=-1, keepdims=True)
    second = jnp.mean(u * xhat, axis=-1, keepdims=True)
    return (u - first - xhat * second) * rstd


def gelu_parts(v):
    size = jnp.abs(v)
    bell = jnp.exp(-0.5 * v * v)
    t = 1.0 / (1.0 + 0.23164188 * size)
    poly = t * (0.127414796 + t * (-0.142248368 + t * (0.71070687 + t * (-0.726576013 + t * 0.530702714))))
    tail = poly * bell
    phi = jnp.where(v < 0, tail, 1.0 - tail)
    return v * phi, phi + (0.3989422804014327 * v) * bell


def ends_of(ref):
    e0 = ref[0, 0]
    e1 = e0 + ref[0, 1]
    return e0, e1, e1 + ref[0, 2]


def segment(position, ends):
    return sum((position >= e).astype(jnp.int32) for e in ends)


def key_features(ref, ends):
    def block(i, _):
        shape = (RB, ref.shape[1])
        seg = segment(lax.broadcasted_iota(jnp.int32, shape, 0) + i * RB, ends)
        lane = lax.broadcasted_iota(jnp.int32, shape, 1)
        ref[rows_of(i), :] = ((lane == seg) | ((lane >= 4) & (lane < 7))).astype(F32).astype(BF16)
        return 0

    lax.fori_loop(0, ref.shape[0] // RB, block, 0)


def query_features(first, count, ends):
    seg = segment(lax.broadcasted_iota(jnp.int32, (16, count), 1) + first, ends)
    row = lax.broadcasted_iota(jnp.int32, (16, count), 0)
    return jnp.where((row < 4) & (row != seg), -FAR, 0.0)


def in_parts(values, row):
    at = lax.broadcasted_iota(jnp.int32, (16, values.shape[1]), 0)
    high = values.astype(BF16).astype(F32)
    middle = (values - high).astype(BF16).astype(F32)
    low = values - high - middle
    return jnp.where(at == row, high, jnp.where(at == row + 1, middle, jnp.where(at == row + 2, low, 0.0)))


def pick(seg, ends, first, last):
    e0, e1, e2 = ends
    start = jnp.where(seg == 0, first, jnp.where(seg == 1, e0, jnp.where(seg == 2, e1, e2)))
    stop = jnp.where(seg == 0, e0, jnp.where(seg == 1, e1, jnp.where(seg == 2, e2, last)))
    return start, stop


NZ, NB = 4, 4
WEIGHTS = 12
SQ, SK, SV, CK, CV, SO, CQ, CO, DOWN, UP, HOUT, HIN = range(WEIGHTS)
VEC = 0
HALVED = (SQ, SK, SV)


def pieces(shapes):
    found = []
    for a, (rows, cols) in enumerate(shapes):
        if rows >= 256:
            found += [(a, j, 4, 0, 1, j > 1) for j in range(4)]
        elif cols >= 4096:
            found += [(a, 0, 1, j, 8, True) for j in range(8)]
        elif a == 1 + SQ:
            found += [(1 + w, 0, 1, h, 2, False) for h in range(2) for w in HALVED]
        elif a - 1 not in HALVED:
            found.append((a, 0, 1, 0, 1, False))
    return found


class Gather:
    RATE = 0.096

    def __init__(self, ins, outs, stages, sems):
        self.ins, self.outs, self.stages = ins, outs, stages
        self.in_s, self.own_s, self.zs, self.zr, self.ws, self.wr, self.ps, self.pr = sems
        self.core, t = lax.axis_index("grp"), lax.axis_index("tok")
        self.z, b = t // NB, t % NB
        y, x = b // 2, b % 2
        by_x, by_y = y * 2 + (1 - x), (1 - y) * 2 + x
        self.b = b
        self.n2 = by_x + self.core * (by_y - by_x)
        self.n3 = by_y + self.core * (by_x - by_y)
        self.pieces = pieces([r.shape for r in ins])
        count = len(self.pieces)
        self.size = []
        for a, _, rn, _, cn, _ in self.pieces:
            rows, cols = ins[a].shape
            self.size.append(NZ * NB * rows * cols * 2 / (rn * cn) / MIB)
        self.now, self.short, self.swaps, self.long = 5.0, 5.0, 0.0, 8.0
        self.next = [0] * 5
        self.detour = [i for i in range(count) if self.pieces[i][5]]
        self.arrive = {}

    def dev(self, core, z, b):
        return {"grp": core, "tok": z * NB + b}

    def peers(self):
        c, z, b = self.core, self.z, self.b
        along = [self.dev(c, (z + d) % NZ, b) for d in (1, 2, 3)]
        return along + [self.dev(c, z, self.n2), self.dev(c, z, self.n3), self.dev(1 - c, z, b)]

    def barrier(self):
        sem = pltpu.get_barrier_semaphore()
        peers = self.peers()
        for p in peers:
            pl.semaphore_signal(sem, inc=1, device_id=p, device_id_type=MESH)
        pl.semaphore_wait(sem, len(peers))

    def cut(self, i):
        a, rj, rn, cj, cn, _ = self.pieces[i]
        rows, cols = self.ins[a].shape
        r, c = rows // (2 * rn), cols // cn
        first = pl.multiple_of(self.core * (rows // 2) + rj * r, r)
        return a, pl.ds(first, r), pl.ds(rj * r, r), pl.ds(cj * c, c)

    def half(self, a):
        rows = self.ins[a].shape[0] // 2
        return pl.ds(pl.multiple_of(self.core * rows, rows), rows)

    def staged(self, a):
        return pltpu.make_async_copy(self.ins[a].at[self.half(a)], self.stages[a], self.in_s.at[a])

    def own(self, a):
        return pltpu.make_async_copy(self.stages[a], self.outs[a].at[self.z, self.b, self.half(a)], self.own_s.at[a])

    def along_z(self, i, d):
        a, r, here, c = self.cut(i)
        return pltpu.make_async_remote_copy(
            self.stages[a].at[here, c], self.outs[a].at[self.z, self.b, r, c],
            self.zs.at[i, d - 1], self.zr.at[i, d - 1],
            device_id=self.dev(self.core, (self.z + d) % NZ, self.b), device_id_type=MESH,
        )

    def aside(self, i):
        a, r, here, c = self.cut(i)
        return pltpu.make_async_remote_copy(
            self.stages[a].at[here, c], self.outs[a].at[self.z, self.b, r, c], self.ps.at[i, 0], self.pr.at[i, 0],
            device_id=self.dev(self.core, self.z, self.n2), device_id_type=MESH,
        )

    def along_z_too(self, i, d):
        a, r, _, c = self.cut(i)
        ref = self.outs[a].at[self.z, self.n2, r, c]
        return pltpu.make_async_remote_copy(
            ref, ref, self.ws.at[i, d - 1], self.wr.at[i, d - 1],
            device_id=self.dev(self.core, (self.z + d) % NZ, self.b), device_id_type=MESH,
        )

    def column(self, i, b, k, to):
        a, r, _, c = self.cut(i)
        ref = self.outs[a].at[:, b, r, c]
        return pltpu.make_async_remote_copy(
            ref, ref, self.ps.at[i, k], self.pr.at[i, k],
            device_id=self.dev(self.core, self.z, to), device_id_type=MESH,
        )

    def second(self, i):
        return self.column(i, self.b, 0, self.n2)

    def third(self, i):
        return self.column(i, self.b, 1, self.n3)

    def onward(self, i):
        return self.column(i, self.n2, 2, self.n3)

    def swap(self, i):
        a, r, _, c = self.cut(i)
        ref = self.outs[a].at[:, :, r, c]
        return pltpu.make_async_remote_copy(
            ref, ref, self.ps.at[i, 3], self.pr.at[i, 3],
            device_id=self.dev(1 - self.core, self.z, self.b), device_id_type=MESH,
        )

    def begin(self):
        here = set()
        for i, piece in enumerate(self.pieces):
            if piece[0] not in here:
                here.add(piece[0])
                self.staged(piece[0]).wait()
                self.own(piece[0]).start()
            for d in (1, 2, 3):
                self.along_z(i, d).start()
            self.long += self.size[i] / 4 / self.RATE
            self.arrive["z", i] = self.long
            if piece[5]:
                self.aside(i).start()
                self.short += self.size[i] / 32 / self.RATE
                self.arrive["aside", i] = self.short + 1

    def ready(self, kind):
        at = self.next[kind]
        if kind == 4:
            return self.arrive["aside", self.detour[at]] if at < len(self.detour) else None
        if at >= len(self.pieces):
            return None
        names = (("z",), ("z2",) if self.pieces[at][5] else ("second",), ("third", "onward"), ("swap",))[kind]
        when = [self.arrive.get((name, at)) for name in names]
        return None if None in when else max(when)

    def event(self, kind):
        self.now = max(self.now, self.ready(kind)) + 0.15
        at = self.next[kind]
        self.next[kind] += 1
        i = self.detour[at] if kind == 4 else at
        a, rj, _, cj, _, detour = self.pieces[i]
        link = self.size[i] / 8 / self.RATE

        def sent(name):
            self.short = max(self.short, self.now) + link
            self.arrive[name, i] = self.short + 1

        if kind == 0:
            if rj == 0 and cj == 0:
                self.own(a).wait()
            for d in (1, 2, 3):
                self.along_z(i, d).wait_recv()
            if not detour:
                self.second(i).start()
                sent("second")
            self.third(i).start()
            sent("third")
        elif kind == 1:
            if detour:
                for d in (1, 2, 3):
                    self.along_z_too(i, d).wait_recv()
            else:
                self.second(i).wait_recv()
            self.onward(i).start()
            sent("onward")
        elif kind == 2:
            self.third(i).wait_recv()
            self.onward(i).wait_recv()
            self.swap(i).start()
            self.swaps = max(self.swaps, self.now) + self.size[i] * 0.86
            self.arrive["swap", i] = self.swaps + 1.5
        elif kind == 3:
            self.swap(i).wait_recv()
        else:
            self.aside(i).wait_recv()
            for d in (1, 2, 3):
                self.along_z_too(i, d).start()
            self.long = max(self.long, self.now) + self.size[i] / 4 / self.RATE
            self.arrive["z2", i] = self.long

    def pump(self):
        going = True
        while going:
            going = False
            for kind in (4, 1, 2, 3, 0):
                when = self.ready(kind)
                if when is not None and when <= self.now and (kind or self.short - self.now < 7):
                    self.event(kind)
                    going = True
                    break

    def passed(self, us):
        self.now += us
        self.pump()

    def until(self, last):
        while self.next[3] <= last:
            self.pump()
            if self.next[3] <= last:
                late = [(self.ready(k) + (max(0, self.short - self.now - 7) if k == 0 else 0), -k) for k in range(5) if self.ready(k) is not None]
                self.event(-min(late)[1])

    def whole(self, a):
        self.until(max(i for i, p in enumerate(self.pieces) if p[0] == a))

    def part(self, a, j):
        self.until([i for i, p in enumerate(self.pieces) if p[0] == a][j])

    def finish(self):
        self.until(len(self.pieces) - 1)
        for i, piece in enumerate(self.pieces):
            for d in (1, 2, 3):
                self.along_z(i, d).wait_send()
                if piece[5]:
                    self.along_z_too(i, d).wait_send()
            for copy in (self.aside if piece[5] else self.second, self.third, self.onward, self.swap):
                copy(i).wait_send()


def gather_scratch(shapes):
    n, k = len(shapes), len(pieces(shapes))
    dma = pltpu.SemaphoreType.DMA
    return [pltpu.VMEM((r // 2, c), BF16) for r, c in shapes] + [dma((n,)), dma((n,)), dma((k, 3)), dma((k, 3)), dma((k, 3)), dma((k, 3)), dma((k, 4)), dma((k, 4))]


SQB, SVB, SOB, G1, S1, CQB, CVB, COB, G2, S2, HOB, G3, S3, AUB = ((p % 2) * 8 + p // 2 for p in range(14))


def pack_vectors(vectors, hidden_bias, down_bias, groups):
    total, at = 0, 0
    for v in (*vectors, hidden_bias, down_bias):
        part = v.reshape(groups, -1) if groups > 1 else v
        more = part.shape[-1]
        total = total + jnp.pad(part, [(0, 0)] * (part.ndim - 1) + [(at, 4096 - at - more)])
        at += more
    return total.reshape(groups, 32, 128)


def unpack_vectors(packed, vec, hidden_bias, down_bias):
    lane = lax.broadcasted_iota(jnp.int32, (16, 128), 1)
    blocks = [packed[t][:16].astype(F32) for t in range(16)]
    turned = [pltpu.roll(b, HEAD, 1) for b in blocks]
    for u in range(8):
        cols = slice(u * 128, (u + 1) * 128)
        vec[0:8, cols] = jnp.where(lane < HEAD, blocks[2 * u], turned[2 * u + 1])[:8]
        vec[8:16, cols] = jnp.where(lane < HEAD, turned[2 * u], blocks[2 * u + 1])[:8]
    for t in range(16):
        for j in range(2):
            first = t * 256 + j * 128
            hidden_bias[:, first : first + 128] = blocks[t][7 + j : 8 + j]
    for u in range(4):
        row = blocks[4 * u]
        for j in range(1, 4):
            row = jnp.where(lane < 32 * j, row, pltpu.roll(blocks[4 * u + j], 32 * j, 1))
        down_bias[:, u * 128 : (u + 1) * 128] = row[9:10]


def attend_block(i, extent, causal, q_t, k, v_t, k_feat, q_feat, mix, mix_t, lse, even, odd, start, pairs):
    cols = pl.ds(i * QB if isinstance(i, int) else pl.multiple_of(i * QB, QB), QB)
    chunks = [(a, min(RB, extent - a)) for a in range(0, extent, RB)]
    empty = jnp.zeros((PAIR - 16, 2 * QB), BF16)

    def step(p, before, now):
        if before is not None:
            peak = jnp.full((8, 2 * QB), -3e38, F32)
            for a, w in chunks:
                peak = jnp.maximum(peak, jnp.max(before[a : a + w, :].reshape(w // 8, 8, 2 * QB), axis=0))
            peak = jnp.max(peak, axis=0, keepdims=True)
            total = jnp.zeros((8, 2 * QB), F32)
            acc = jnp.zeros((PAIR, 2 * QB), F32)
        if now is not None:
            wide = jnp.concatenate([two_heads(q_t[lanes_of(p + 1), cols]), twice(q_feat[:, cols]), empty], axis=0)
        for a, w in chunks:
            if now is not None:
                s = dot(jnp.concatenate([k[a : a + w, lanes_of(p + 1)], k_feat[a : a + w, :]], axis=1), wide)
                if causal and a + w == extent:
                    key = lax.broadcasted_iota(jnp.int32, (w, 2 * QB), 0) + a
                    query = lax.broadcasted_iota(jnp.int32, (w, 2 * QB), 1) % QB + i * QB
                    s = jnp.where(key <= query, s, -FAR)
                now[a : a + w, :] = s
            if before is not None:
                e = jnp.exp(before[a : a + w, :] - peak)
                total = total + jnp.sum(e.reshape(w // 8, 8, 2 * QB), axis=0)
                acc = acc + dot(v_t[lanes_of(p), a : a + w], e.astype(BF16))
        if before is not None:
            total = jnp.sum(total, axis=0, keepdims=True)
            out = one_of_each(acc * (1.0 / total)).astype(BF16)
            mix_t[lanes_of(p), cols] = out
            mix[cols, lanes_of(p)] = jnp.transpose(out)
            both = peak + jnp.log(total)
            lse[p, 0:1, cols] = both[:, :QB]
            lse[p, 1:2, cols] = both[:, QB:]

    def loop(g, _):
        step(start + 2 * g, even, odd)
        step(start + 2 * g + 1, odd, even)
        return 0

    step(start - 1, None, even)
    lax.fori_loop(0, pairs // 2 - 1, loop, 0)
    step(start + pairs - 2, even, odd)
    step(start + pairs - 1, odd, None)


SAVED = 16
(O_SQ, O_SK, O_SV, O_SM, O_CQ, O_CK, O_CV, O_CM, O_XH1, O_XH2, O_X2B, O_DH, O_DB, O_AB, O_R3, O_STAT) = range(SAVED)


def forward_kernel(remote, *refs):
    tokens, enc, dec_len, enc_len = refs[:4]
    arrays, refs = refs[4 : 5 + WEIGHTS], refs[5 + WEIGHTS :]
    gather = None
    if remote:
        extra = len(arrays) + 8
        gather = Gather(arrays, refs[: 1 + WEIGHTS], refs[-extra:-8], refs[-8:])
        arrays, refs = refs[: 1 + WEIGHTS], refs[1 + WEIGHTS : -extra]

    saved = refs[:SAVED]
    lse1, lse2, vec = refs[SAVED : SAVED + 3]
    (pool, even, odd, kf1, kf2, qf, xf, wslots, oslots, aslots, dbot, abot, stat, packed, hb, db, pool_s, w_s, out_s) = refs[SAVED + 3 :]
    X, ENC, QS, KS, VS, KC, VC, MIX, MTS, X1B, XH1, QC, MTC, X2B, XH2 = range(15)
    VTS, VTC = XH1, XH2
    DG = (X, ENC, KC, VC)
    n_rows = pool.shape[1] // RB

    loads = [pltpu.make_async_copy(tokens, pool.at[X], pool_s.at[0]), pltpu.make_async_copy(enc, pool.at[ENC], pool_s.at[1])]
    if gather is not None:
        for a in range(len(arrays)):
            gather.staged(a).start()
    for c in loads:
        c.start()
    if gather is not None:
        gather.barrier()
        gather.begin()

    free_slots = wslots.shape[0]
    fetches, slot_of = {}, {}
    for h in range(2):
        for k, w in enumerate(HALVED):
            at = slice(h * 512, (h + 1) * 512)
            fetches[w, h], slot_of[w, h] = (arrays[1 + w].at[:, :, :, at], wslots.at[k, :, :, :, at]), (0, k, h)
    for k, w in enumerate((CK, CV, SO, CQ, CO), 3):
        fetches[w], slot_of[w] = (arrays[1 + w], wslots.at[k % free_slots]), (0, k % free_slots, None)
    for k, w in enumerate((DOWN, UP)):
        fetches[w], slot_of[w] = (arrays[1 + w], aslots.at[k]), (1, k, None)
    for j in range(4):
        for h in range(2):
            if h == 0:
                fetches[HOUT, j] = (arrays[1 + HOUT].at[j], oslots.at[j % oslots.shape[0]])
                slot_of[HOUT, j] = (2, j % oslots.shape[0], None)
            at = slice(h * 512, (h + 1) * 512)
            source = arrays[1 + HIN].at[:, :, :, j * 1024 + h * 512 : j * 1024 + (h + 1) * 512]
            fetches[HIN, 2 * j + h] = (source, wslots.at[j % free_slots, :, :, :, at])
            slot_of[HIN, 2 * j + h] = (0, j % free_slots, h)
    order = list(fetches)

    def copy_of(k):
        return pltpu.make_async_copy(*fetches[k], w_s.at[order.index(k)])

    started, used = [], set()

    def arrived(k):
        return gather is None or gather.next[3] > piece_of(k)

    def piece_of(k):
        a, j = (k, None) if isinstance(k, int) else k
        found = [i for i, p in enumerate(gather.pieces) if p[0] == 1 + a]
        return found[-1] if j is None or a == HOUT else found[j]

    def ahead(k):
        kind, slot, half = slot_of[k]
        before = [u for u in order[: order.index(k)] if slot_of[u][:2] == (kind, slot)]
        return all(u in used for u in before if half is None or slot_of[u][2] in (None, half))

    def prefetch():
        while len(started) < len(order) and arrived(order[len(started)]) and ahead(order[len(started)]):
            copy_of(order[len(started)]).start()
            started.append(order[len(started)])

    def passed(us):
        if gather is not None:
            gather.passed(us)
        prefetch()

    def weight(k):
        if gather is not None:
            gather.until(piece_of(k))
        prefetch()
        assert k in started
        copy_of(k).wait()
        ref = fetches[k][1]
        return lambda: ref[...].reshape(-1, ref.shape[-1])

    writes = []

    def write(src, slot, dst=None):
        c = pltpu.make_async_copy(src, saved[slot] if dst is None else dst, out_s.at[len(writes)])
        c.start()
        writes.append(c)

    dec_ends, enc_ends = ends_of(dec_len), ends_of(enc_len)
    key_features(kf1, dec_ends)
    key_features(kf2, enc_ends)
    qf[...] = query_features(0, qf.shape[1], dec_ends).astype(BF16)
    if gather is not None:
        gather.whole(VEC)
    packed_in = pltpu.make_async_copy(arrays[VEC], packed, pool_s.at[2])
    packed_in.start()
    packed_in.wait()
    unpack_vectors([packed[t // NB, t % NB] for t in range(NZ * NB)], vec, hb, db)
    for c in loads:
        c.wait()

    def project(src, w, dst, b=None, factor=None, turned=None, at=slice(0, 1024)):
        get = weight(w)

        def block(i, _):
            r = dot(pool[src, rows_of(i), :], get())
            if b is not None:
                r = r + vec[b : b + 1, at]
            r = r.astype(BF16)
            if factor is not None:
                r = r * jnp.asarray(factor, BF16)
            if dst is not None:
                pool[dst, rows_of(i), at] = r
            if turned is not None:
                pool[turned, at, rows_of(i)] = jnp.transpose(r)
            return 0

        lax.fori_loop(0, n_rows, block, 0)
        used.add(w)
        passed(3 * (at.stop - at.start) / 1024)

    shrink = HEAD ** (-0.5)
    n_blocks = pool.shape[1] // QB
    for h in range(2):
        at = slice(h * 512, (h + 1) * 512)
        project(X, (SQ, h), None, SQB, shrink, QS, at)
        project(X, (SK, h), KS, at=at)
        project(X, (SV, h), VS, SVB, None, VTS, at)
        if h == 1:
            write(pool.at[QS], O_SQ)
            write(pool.at[KS], O_SK)
            write(pool.at[VS], O_SV)
        for i in range(n_blocks):
            attend_block(i, (i + 1) * QB, True, pool.at[QS], pool.at[KS], pool.at[VTS], kf1, qf, pool.at[MIX], pool.at[MTS], lse1, even, odd, 4 * h, 4)
            passed(0.33 * (i + 1))
    write(pool.at[MTS], O_SM)
    project(ENC, CK, KC)
    project(ENC, CV, VC, CVB, None, VTC)
    write(pool.at[KC], O_CK)
    write(pool.at[VC], O_CV)

    def mix_out(mixed, w, b, residual, gain, shift, low_slot, hat_slot, column):
        get = weight(w)

        def block(i, _):
            r = residual(i) + dot(pool[mixed, rows_of(i), :], get()) + vec[b : b + 1, :]
            xhat, rstd = normalized(r)
            y = xhat * vec[gain : gain + 1, :] + vec[shift : shift + 1, :]
            xf[rows_of(i), :] = y
            pool[low_slot, rows_of(i), :] = y.astype(BF16)
            pool[hat_slot, rows_of(i), :] = xhat.astype(BF16)
            stat[column, rows_of(i), :] = jnp.broadcast_to(rstd, (RB, 128))
            return 0

        lax.fori_loop(0, n_rows, block, 0)
        used.add(w)
        passed(4)

    mix_out(MIX, SO, SOB, lambda i: pool[X, rows_of(i), :].astype(F32), G1, S1, X1B, XH1, 0)
    write(pool.at[XH1], O_XH1)
    project(X1B, CQ, None, CQB, shrink, QC)
    write(pool.at[QC], O_CQ)
    for part in range(4):

        def block(i, _):
            attend_block(i, pool.shape[1], False, pool.at[QC], pool.at[KC], pool.at[VTC], kf2, qf, pool.at[MIX], pool.at[MTC], lse2, even, odd, 0, 8)
            return 0

        lax.fori_loop(part * n_blocks // 4, (part + 1) * n_blocks // 4, block, 0)
        passed(8)
    write(pool.at[MTC], O_CM)
    mix_out(MIX, CO, COB, lambda i: xf[rows_of(i), :], G2, S2, X2B, XH2, 1)
    write(pool.at[XH2], O_XH2)
    write(pool.at[X2B], O_X2B)
    write(stat, O_STAT)

    down, up = weight(DOWN), weight(UP)

    def adapter(i, _):
        pre = dot_nt(pool[X2B, rows_of(i), :], down()) + db[...]
        act, slope = gelu_parts(pre)
        low = act.astype(BF16)
        abot[rows_of(i), :] = low
        dbot[rows_of(i), :] = slope.astype(BF16)
        more = dot(low, up()) + vec[AUB : AUB + 1, :]
        xf[rows_of(i), :] = xf[rows_of(i), :] + vec[HOB : HOB + 1, :] + SCALE * more
        return 0

    lax.fori_loop(0, n_rows, adapter, 0)
    passed(5)
    write(abot, O_AB)
    write(dbot, O_DB)
    for c in writes[:7]:
        c.wait()
    for j in range(8):
        if j % 2 == 0:
            w_out = weight((HOUT, j // 2))
        w_in = weight((HIN, j))
        at, rows_at = slice(j * 512, (j + 1) * 512), slice(j % 2 * 512, j % 2 * 512 + 512)

        def into(i, w_in=w_in, at=at):
            return dot(pool[X2B, rows_of(i), :], w_in()) + hb[:, at]

        def out_of(i, pre, j=j, w_out=w_out, rows_at=rows_at):
            act, slope = gelu_parts(pre)
            pool[DG[j // 2], rows_of(i), rows_at] = slope.astype(BF16)
            xf[rows_of(i), :] = xf[rows_of(i), :] + dot(act.astype(BF16), w_out()[rows_at, :])

        def hidden(g, _):
            first, second = into(2 * g), into(2 * g + 1)
            out_of(2 * g, first)
            out_of(2 * g + 1, second)
            return 0

        lax.fori_loop(0, n_rows // 2, hidden, 0)
        used.add((HIN, j))
        if j % 2:
            used.add((HOUT, j // 2))
        passed(4.5)
        if j % 2:
            half = j // 2
            write(pool.at[DG[half]], O_DH, saved[O_DH].at[:, half * 1024 : (half + 1) * 1024])
    write(xf, O_R3)
    for c in writes[7:]:
        c.wait()
    if gather is not None:
        gather.finish()


def forward(tokens, enc, dec_len, enc_len, arrays, remote):
    slots, width = tokens.shape
    hidden = arrays[1 + HIN].shape[-1]
    bottle = arrays[1 + DOWN].size // width * (NZ * NB if remote else 1)
    bf, f3 = functools.partial(jax.ShapeDtypeStruct, dtype=BF16), functools.partial(jax.ShapeDtypeStruct, dtype=F32)
    main = bf((slots, width))
    outs = [main] * 11 + [bf((slots, hidden)), bf((slots, bottle)), bf((slots, bottle)), f3((slots, width)), f3((2, slots, 128))]
    outs += [f3((width // PAIR, 2, slots)), f3((width // PAIR, 2, slots)), f3((16, width))]
    gathered = [bf((NZ, NB) + a.shape) for a in arrays] if remote else []
    params = dict(collective_id=0, has_side_effects=True) if remote else {}
    kept = pl.pallas_call(
        functools.partial(forward_kernel, remote),
        out_shape=gathered + outs,
        in_specs=[ANY, ANY, SMEM, SMEM] + [ANY] * len(arrays),
        out_specs=[ANY] * (len(gathered) + SAVED) + [WHOLE] * 3,
        scratch_shapes=[
            pltpu.VMEM((15, slots, width), BF16),
            pltpu.VMEM((slots, 2 * QB), F32),
            pltpu.VMEM((slots, 2 * QB), F32),
            pltpu.VMEM((slots, PAIR), BF16),
            pltpu.VMEM((slots, PAIR), BF16),
            pltpu.VMEM((16, slots), BF16),
            pltpu.VMEM((slots, width), F32),
            pltpu.VMEM((4, NZ, NB, 64, 1024), BF16),
            pltpu.VMEM((2, NB, 256, 1024), BF16),
            pltpu.VMEM((2, NZ, NB, bottle // 16, 1024), BF16),
            pltpu.VMEM((slots, bottle), BF16),
            pltpu.VMEM((slots, bottle), BF16),
            pltpu.VMEM((2, slots, 128), F32),
            pltpu.VMEM((NZ, NB, 32, 128), BF16),
            pltpu.VMEM((1, hidden), F32),
            pltpu.VMEM((1, bottle), F32),
            pltpu.SemaphoreType.DMA((3,)),
            pltpu.SemaphoreType.DMA((32,)),
            pltpu.SemaphoreType.DMA((24,)),
        ] + (gather_scratch([a.shape for a in arrays]) if remote else []),
        compiler_params=pltpu.CompilerParams(vmem_limit_bytes=VMEM, **params),
        cost_estimate=cost(slots * (16 * width * width + 4 * slots * width * 8), *arrays, *outs),
        name="forward",
    )(tokens, enc, dec_len, enc_len, *arrays)
    return (kept[: len(gathered)] or list(arrays)), kept[len(gathered) :]


def head_sums(grad_t, mix_t):
    product = grad_t.astype(F32) * mix_t.astype(F32)
    return jnp.sum(product.reshape(-1, HEAD, product.shape[1]), axis=1)


def head_back_kernel(dec_len, r3, cot, vec, db, ab, x2b, down, up, out, g3, g3b, grads, gbias):
    i = pl.program_id(0)
    ends = ends_of(dec_len)
    xhat, rstd = normalized(r3[...])
    gain = vec[G3 : G3 + 1, :]
    out[...] = (xhat * gain + vec[S3 : S3 + 1, :]).astype(BF16)
    pos = lax.broadcasted_iota(jnp.int32, r3.shape, 0) + i * r3.shape[0]
    upstream = jnp.where(pos < ends[2], cot[...].astype(F32), 0.0)
    g = norm_back(xhat, rstd, gain, upstream)
    g3b[...] = g.astype(BF16)
    g_adapt = (SCALE * g).astype(BF16)
    g_bottle = (db[...].astype(F32) * dot_nt(g_adapt, up[...])).astype(BF16)
    g3[...] = g + dot(g_bottle, down[...])

    @pl.when(i == 0)
    def _():
        grads[...] = jnp.zeros_like(grads)
        gbias[...] = jnp.zeros_like(gbias)

    grads[0] = grads[0] + dot_tn(g_bottle, x2b[...])
    grads[1] = grads[1] + dot_tn(ab[...], g_adapt)
    gbias[0:1, :] = gbias[0:1, :] + jnp.sum(g_adapt.astype(F32), axis=0, keepdims=True)
    wide = gbias[1:2, 0 : db.shape[1]]
    gbias[1:2, 0 : db.shape[1]] = wide + jnp.sum(g_bottle.astype(F32), axis=0, keepdims=True)


def full(shape):
    return pl.BlockSpec(shape, lambda *_: (0,) * len(shape))


def head_back(dec_len, r3, cot, vec, db, ab, x2b, down, up):
    slots, width = r3.shape
    bottle = db.shape[1]
    sds = jax.ShapeDtypeStruct
    row, low = pl.BlockSpec((RB, width), lambda i: (i, 0)), pl.BlockSpec((RB, bottle), lambda i: (i, 0))
    outs = [
        sds((slots, width), BF16), sds((slots, width), F32), sds((slots, width), BF16),
        sds((2, bottle, width), F32), sds((8, width), F32),
    ]
    return pl.pallas_call(
        head_back_kernel,
        grid=(slots // RB,),
        out_shape=outs,
        in_specs=[SMEM, row, row, full(vec.shape), low, low, row, full(down.shape), full(up.shape)],
        out_specs=[row] * 3 + [full(o.shape) for o in outs[3:]],
        compiler_params=pltpu.CompilerParams(vmem_limit_bytes=VMEM),
        cost_estimate=cost(slots * 4 * width * bottle, *outs, r3, cot),
        name="head_back",
    )(dec_len, r3, cot, vec, db, ab, x2b, down, up)


class Reduce:
    def __init__(self, grads, gbias, shares, bias, scratch):
        self.grads, self.gbias, self.shares, self.bias = grads, gbias, shares, bias
        (self.s1, self.r1, self.s2, self.r2, self.s3, self.r3, self.s4, self.r4, self.f5, self.r5,
         self.sb, self.rb, self.acc2, self.acc3, self.send, self.recv) = scratch
        self.core, t = lax.axis_index("grp"), lax.axis_index("tok")
        self.z, b = t // NB, t % NB
        self.y, self.x = b // 2, b % 2
        self.b = b
        by_x, by_y = self.y * 2 + (1 - self.x), (1 - self.y) * 2 + self.x
        core, z = self.core, self.z
        n2, n3 = by_x + core * (by_y - by_x), by_y + core * (by_x - by_y)
        self.across = {"grp": 1 - core, "tok": t}
        self.second = {"grp": core, "tok": z * NB + n2}
        self.third = {"grp": core, "tok": z * NB + n3}
        self.along = [{"grp": core, "tok": (z + d) % NZ * NB + b} for d in (1, 2, 3)]

    def copy(self, n, src, dst, to):
        return pltpu.make_async_remote_copy(src, dst, self.send.at[n], self.recv.at[n], device_id=to, device_id_type=MESH)

    def copies(self, stage):
        if stage == 1:
            return [self.copy(0, self.s1, self.r1, self.across), self.copy(1, self.sb.at[0], self.rb.at[0], self.across)]
        if stage == 2:
            return [self.copy(2, self.s2, self.r2, self.second), self.copy(3, self.sb.at[1], self.rb.at[1], self.second)]
        if stage == 3:
            return [self.copy(4, self.s3, self.r3, self.third), self.copy(5, self.sb.at[2], self.rb.at[2], self.third)]
        if stage == 4:
            moves = [self.copy(6 + d, self.s4.at[d], self.r4.at[d], self.along[d]) for d in range(3)]
            return moves + [self.copy(9 + d, self.sb.at[3], self.rb.at[3 + d], self.along[d]) for d in range(3)]
        return [self.copy(12, self.f5, self.r5, self.across)]

    def go(self, stage):
        for c in self.copies(stage):
            c.start()

    def wait(self, stage):
        for c in self.copies(stage):
            c.wait()

    def begin(self):
        sem = pltpu.get_barrier_semaphore()
        for peer in [self.across, self.second, self.third, *self.along]:
            pl.semaphore_signal(sem, inc=1, device_id=peer, device_id_type=MESH)
        pl.semaphore_wait(sem, 6)
        self.s1[...] = self.grads[1 - self.core].astype(BF16)
        self.bias[...] = jnp.concatenate([self.gbias[...], jnp.zeros_like(self.gbias[...])], axis=0)
        self.sb[0] = self.bias[...].astype(BF16)
        self.go(1)

    def add_bias(self, n, more):
        self.bias[...] = self.bias[...] + more
        self.sb[n] = self.bias[...].astype(BF16)

    def first(self):
        self.wait(1)
        total = self.grads[self.core] + self.r1[...].astype(F32)
        rows, width = total.shape[0] // (NZ * NB), total.shape[1]
        total = total.reshape(NZ, 2, 2, rows, width)
        by_x = [total[:, :, k].reshape(2 * NZ, rows, width) for k in range(2)]
        by_y = [total[:, k].reshape(2 * NZ, rows, width) for k in range(2)]
        even, odd = [jnp.where(self.core == 0, u, v) for u, v in zip(by_x, by_y)]
        high = jnp.where(self.core == 0, self.x, self.y) == 1
        self.acc2[...] = jnp.where(high, odd, even)
        self.s2[...] = jnp.where(high, even, odd).astype(BF16)
        self.add_bias(1, self.rb[0].astype(F32))
        self.go(2)

    def next(self):
        self.wait(2)
        total = self.acc2[...] + self.r2[...].astype(F32)
        total = total.reshape((NZ, 2) + total.shape[1:])
        high = jnp.where(self.core == 0, self.y, self.x) == 1
        self.acc3[...] = jnp.where(high, total[:, 1], total[:, 0])
        self.s3[...] = jnp.where(high, total[:, 0], total[:, 1]).astype(BF16)
        self.add_bias(2, self.rb[1].astype(F32))
        self.go(3)

    def then(self):
        self.wait(3)
        self.acc3[...] = self.acc3[...] + self.r3[...].astype(F32)
        for d in range(3):
            self.s4[d] = self.acc3[(self.z + d + 1) % NZ].astype(BF16)
        self.add_bias(3, self.rb[2].astype(F32))
        self.go(4)

    def last(self):
        self.wait(4)
        total = self.acc3[self.z]
        for d in range(3):
            total = total + self.r4[d].astype(F32)
        self.bias[...] = self.bias[...] + self.rb[3].astype(F32) + self.rb[4].astype(F32) + self.rb[5].astype(F32)
        self.f5[...] = total
        self.shares[self.core] = total
        self.go(5)

    def end(self):
        self.wait(5)
        self.shares[1 - self.core] = self.r5[...]


def reduce_scratch(bottle, width):
    vmem, rows = pltpu.VMEM, bottle // (NZ * NB)
    pairs = [(NZ * NB,), (2 * NZ,), (NZ,), (3,)]
    bufs = [vmem((bottle, width), BF16)] * 2
    for lead in pairs[1:]:
        bufs += [vmem(lead + (rows, width), BF16)] * 2
    bufs += [vmem((rows, width), F32)] * 2
    bufs += [vmem((4, 16, width), BF16), vmem((6, 16, width), BF16)]
    bufs += [vmem((2 * NZ, rows, width), F32), vmem((NZ, rows, width), F32)]
    return bufs + [pltpu.SemaphoreType.DMA((13,))] * 2


def ffn_back_kernel(remote, vec, g3b, dh, w_out, w_in, grads, gbias, g3, xh2, stat, cm, co, gr2, gmix, delta, shares, bias,
                    acc, g3_v, xh2_v, stat_v, cm_v, co_v, sems, *scratch):
    step = pl.program_id(0)
    n_rows = g3b.shape[0] // RB
    if remote:
        reduce = Reduce(grads, gbias, shares, bias, scratch)
        for n, part in enumerate((reduce.begin, reduce.first, reduce.next, reduce.then)):
            pl.when(step == n)(part)
    moves = [(g3, g3_v), (xh2, xh2_v), (stat, stat_v), (cm, cm_v), (co, co_v)]
    copies = [pltpu.make_async_copy(a, b, sems.at[n]) for n, (a, b) in enumerate(moves)]

    @pl.when(step == 0)
    def _():
        for c in copies:
            c.start()
        acc[...] = jnp.zeros_like(acc)

    def hidden(i, _):
        blocks = [rows_of(2 * i), rows_of(2 * i + 1)]
        pres = [dot_nt(g3b[rows, :], w_out[...]) for rows in blocks]
        for rows, pre in zip(blocks, pres):
            g = (dh[rows, :].astype(F32) * pre).astype(BF16)
            acc[rows, :] = acc[rows, :] + dot_nt(g, w_in[...])
        return 0

    lax.fori_loop(0, n_rows // 2, hidden, 0)

    @pl.when(step == pl.num_programs(0) - 1)
    def _():
        if remote:
            reduce.last()
        for c in copies:
            c.wait()

        def last(i, _):
            rows = rows_of(i)
            g = acc[rows, :] + g3_v[rows, :]
            g = norm_back(xh2_v[rows, :].astype(F32), stat_v[1, rows, 0:1], vec[G2 : G2 + 1, :], g)
            gr2[rows, :] = g
            mix = dot_nt(co_v[...], g.astype(BF16)).astype(BF16)
            gmix[:, rows] = mix
            delta[:, rows] = head_sums(mix, cm_v[:, rows])
            return 0

        lax.fori_loop(0, n_rows, last, 0)
        if remote:
            reduce.end()


def ffn_back(remote, vec, g3b, dh, w_out, w_in, grads, gbias, g3, xh2, stat, cm, co):
    slots, width = g3.shape
    hidden = dh.shape[1]
    step = 1024
    sds = jax.ShapeDtypeStruct
    bottle = grads.shape[1]
    outs = [sds((slots, width), F32), sds((width, slots), BF16), sds((width // HEAD, slots), F32)]
    outs += [sds((2, bottle // (NZ * NB), width), F32), sds((16, width), F32)]
    late = [g3, xh2, stat, cm, co]
    params = dict(collective_id=1, has_side_effects=True) if remote else {}
    return pl.pallas_call(
        functools.partial(ffn_back_kernel, remote),
        grid=(hidden // step,),
        out_shape=outs,
        in_specs=[
            full(vec.shape), full(g3b.shape),
            pl.BlockSpec((slots, step), lambda c: (0, c)),
            pl.BlockSpec((step, width), lambda c: (c, 0)),
            pl.BlockSpec((width, step), lambda c: (0, c)),
            full(grads.shape), full(gbias.shape),
        ] + [ANY] * len(late),
        out_specs=[full(o.shape) for o in outs],
        scratch_shapes=[pltpu.VMEM((slots, width), F32)]
        + [pltpu.VMEM(a.shape, a.dtype) for a in late]
        + [pltpu.SemaphoreType.DMA((len(late),))]
        + (reduce_scratch(bottle, width) if remote else []),
        compiler_params=pltpu.CompilerParams(vmem_limit_bytes=VMEM, **params),
        cost_estimate=cost(slots * width * (2 * hidden + width), *outs, dh, w_out, w_in, co),
        name="ffn_back",
    )(vec, g3b, dh, w_out, w_in, grads, gbias, *late)


def cross_tail(i, dq, dk, dv, vec, gr2, xh1, stat, sm, cq, ck, cv, so, genc, gmix, delta):
    rows = rows_of(i)
    genc[rows, :] = (dot_nt(dk[rows, :], ck[...]) + dot_nt(dv[rows, :], cv[...])).astype(BF16)
    g = gr2[rows, :] + dot_nt(dq[rows, :], cq[...])
    g = norm_back(xh1[rows, :].astype(F32), stat[0, rows, 0:1], vec[G1 : G1 + 1, :], g)
    gr2[rows, :] = g
    mix = dot_nt(so[...], g.astype(BF16)).astype(BF16)
    gmix[:, rows] = mix
    delta[:, rows] = head_sums(mix, sm[:, rows])


def self_tail(i, dq, dk, dv, gr1, sq, sk, sv, gtok):
    rows = rows_of(i)
    g = gr1[rows, :] + dot_nt(dq[rows, :], sq[...]) + dot_nt(dk[rows, :], sk[...]) + dot_nt(dv[rows, :], sv[...])
    gtok[rows, :] = g.astype(BF16)


def attend_back_kernel(causal, q_len, k_len, q_t, k, v, g_t, lse, delta, *rest):
    if causal:
        late, outs, rest = rest[:4], rest[4:5], rest[5:]
        late_v, staged, rest = rest[:4], rest[4:5], rest[5:]
    else:
        vec, late, outs, new_delta, rest = rest[0], rest[1:9], rest[9:12], rest[12], rest[13:]
        late_v, staged, rest = rest[:8], rest[8:10], rest[10:]
    (dq, dk, dv, late_s, out_s, dk_t, dv_t, dq_t, k_t, qx, gx, kf, s_buf, d_buf, tile_i, tile_j, new_q, new_k, tiles) = rest
    step = pl.program_id(0)

    @pl.when(step == 0)
    def _():
        for n, (src, dst) in enumerate(zip(late, late_v)):
            pltpu.make_async_copy(src, dst, late_s.at[n]).start()

    slots, pairs = k.shape[0], k.shape[1] // PAIR
    blocks = slots // QB
    q_ends, k_ends = ends_of(q_len), ends_of(k_len)

    @pl.when(pl.program_id(0) == 0)
    def _():
        key_features(kf, k_ends)
        count = jnp.int32(0)
        reached = jnp.int32(0)
        for i in range(blocks):
            low, _ = pick(segment(jnp.int32(i * QB), q_ends), k_ends, 0, slots)
            _, high = pick(segment(jnp.int32(i * QB + QB - 1), q_ends), k_ends, 0, slots)
            if causal:
                high = jnp.minimum(high, (i + 1) * QB)

            def put(j, n, i=i, low=low, reached=reached):
                tile_i[n] = i
                tile_j[n] = j
                new_q[n] = (j == low // KB).astype(jnp.int32)
                new_k[n] = (j >= reached).astype(jnp.int32)
                return n + 1

            count = lax.fori_loop(low // KB, (high + KB - 1) // KB, put, count)
            reached = jnp.maximum(reached, (high + KB - 1) // KB)
        tiles[0] = count

    k_t[...] = jnp.transpose(k[...])
    empty = jnp.zeros((PAIR - 16, 2 * QB), BF16)
    for i in range(blocks):
        cols = slice(i * QB, (i + 1) * QB)
        far = twice(query_features(i * QB, QB, q_ends))
        for n in range(pairs):
            part = slice(n * PAIR, (n + 1) * PAIR)
            both_lse = jnp.concatenate([lse[n, 0:1, cols], lse[n, 1:2, cols]], axis=1)
            both_delta = jnp.concatenate([delta[2 * n : 2 * n + 1, cols], delta[2 * n + 1 : 2 * n + 2, cols]], axis=1)
            qx[n, i, :PAIR, :] = two_heads(q_t[part, cols])
            qx[n, i, PAIR : PAIR + 16, :] = (far + in_parts(-both_lse, 4)).astype(BF16)
            qx[n, i, PAIR + 16 :, :] = empty
            gx[n, i, :PAIR, :] = two_heads(g_t[part, cols])
            gx[n, i, PAIR : PAIR + 16, :] = in_parts(-both_delta, 4).astype(BF16)
            gx[n, i, PAIR + 16 :, :] = empty

    if causal:
        shape = (KB, 2 * QB)
        ahead = lax.broadcasted_iota(jnp.int32, shape, 0) - lax.broadcasted_iota(jnp.int32, shape, 1) % QB

    def keys_of(j):
        return pl.ds(pl.multiple_of(j * KB, KB), KB)

    def scores(t, n):
        i, keys = tile_i[t], keys_of(tile_j[t])
        part = slice(n * PAIR, (n + 1) * PAIR)
        s_buf[n] = dot(jnp.concatenate([k[keys, part], kf[keys, :]], axis=1), qx[n, i])
        d_buf[n] = dot(jnp.concatenate([v[keys, part], kf[keys, :]], axis=1), gx[n, i])

    def grads(t, n):
        i, j = tile_i[t], tile_j[t]
        keys = keys_of(j)
        p = jnp.exp(s_buf[n])
        if causal:
            p = jnp.where(ahead <= i * QB - j * KB, p, 0.0)
        d = (p * d_buf[n]).astype(BF16)
        first_q, first_k = new_q[t] == 1, new_k[t] == 1
        dv_t[n, :, keys] = jnp.where(first_k, 0.0, dv_t[n, :, keys]) + dot_nt(gx[n, i, :PAIR, :], p.astype(BF16))
        dk_t[n, :, keys] = jnp.where(first_k, 0.0, dk_t[n, :, keys]) + dot_nt(qx[n, i, :PAIR, :], d)
        dq_t[n, i] = jnp.where(first_q, 0.0, dq_t[n, i]) + dot(k_t[n * PAIR : (n + 1) * PAIR, keys], d)

    def loop(t, _):
        for n in range(pairs):
            grads(t - 1, n)
            scores(t, n)
        return 0

    last = tiles[0]
    for n in range(pairs):
        scores(0, n)
    lax.fori_loop(1, last, loop, 0)
    for n in range(pairs):
        grads(last - 1, n)
    for n in range(pairs):
        part = pl.ds(pl.multiple_of((step * pairs + n) * PAIR, PAIR), PAIR)
        dk[:, part] = jnp.transpose(dk_t[n].astype(BF16))
        dv[:, part] = jnp.transpose(dv_t[n].astype(BF16))
        for i in range(blocks):
            dq[i * QB : (i + 1) * QB, part] = jnp.transpose((one_of_each(dq_t[n, i]) * HEAD ** (-0.5)).astype(BF16))

    @pl.when(step == pl.num_programs(0) - 1)
    def _():
        for n, (src, dst) in enumerate(zip(late, late_v)):
            pltpu.make_async_copy(src, dst, late_s.at[n]).wait()
        results = [*staged] if causal else [staged[0], late_v[0], staged[1]]

        def back(n, i):
            at = (slice(None), rows_of(i)) if n == 2 else (rows_of(i), slice(None))
            return pltpu.make_async_copy(results[n].at[at], outs[n].at[at], out_s.at[n, i])

        def tail(i, _):
            if causal:
                self_tail(i, dq, dk, dv, *late_v, staged[0])
            else:
                cross_tail(i, dq, dk, dv, vec, *late_v, *staged, new_delta)
            for n in range(len(outs)):
                back(n, i).start()
            return 0

        lax.fori_loop(0, slots // RB, tail, 0)
        for i in range(slots // RB):
            for n in range(len(outs)):
                back(n, i).wait()


def attend_back(causal, q_len, k_len, q_t, k, v, g_t, lse, delta, vec, late, group=4):
    slots, width = k.shape
    pairs, blocks, heads = width // PAIR, slots // QB, width // HEAD
    col = pl.BlockSpec((slots, group * PAIR), lambda p: (0, p))
    row = pl.BlockSpec((group * PAIR, slots), lambda p: (p, 0))
    stat = pl.BlockSpec((group, 2, slots), lambda p: (p, 0, 0))
    vmem, sds = pltpu.VMEM, jax.ShapeDtypeStruct
    outs, specs, staged = [sds((slots, width), BF16)], [ANY], [vmem((slots, width), BF16)]
    extra, extra_specs = [], []
    if not causal:
        outs += [sds((slots, width), F32), sds((width, slots), BF16), sds((heads, slots), F32)]
        specs += [ANY, ANY, full((heads, slots))]
        staged += [vmem((width, slots), BF16)]
        extra, extra_specs = [vec], [full(vec.shape)]
    return pl.pallas_call(
        functools.partial(attend_back_kernel, causal),
        grid=(pairs // group,),
        out_shape=outs,
        in_specs=[SMEM, SMEM, row, col, col, row, stat, pl.BlockSpec((2 * group, slots), lambda p: (p, 0))]
        + extra_specs + [ANY] * len(late),
        out_specs=specs,
        scratch_shapes=[vmem(a.shape, a.dtype) for a in late] + staged + [
            vmem((slots, width), BF16),
            vmem((slots, width), BF16),
            vmem((slots, width), BF16),
            pltpu.SemaphoreType.DMA((len(late),)),
            pltpu.SemaphoreType.DMA((3, slots // RB)),
            vmem((group, PAIR, slots), F32),
            vmem((group, PAIR, slots), F32),
            vmem((group, blocks, PAIR, 2 * QB), F32),
            vmem((group * PAIR, slots), BF16),
            vmem((group, blocks, 2 * PAIR, 2 * QB), BF16),
            vmem((group, blocks, 2 * PAIR, 2 * QB), BF16),
            vmem((slots, PAIR), BF16),
            vmem((group, KB, 2 * QB), F32),
            vmem((group, KB, 2 * QB), F32),
            pltpu.SMEM((blocks * blocks,), jnp.int32),
            pltpu.SMEM((blocks * blocks,), jnp.int32),
            pltpu.SMEM((blocks * blocks,), jnp.int32),
            pltpu.SMEM((blocks * blocks,), jnp.int32),
            pltpu.SMEM((1,), jnp.int32),
        ],
        compiler_params=pltpu.CompilerParams(vmem_limit_bytes=VMEM),
        cost_estimate=cost(5 * slots * slots * width * 4 + 4 * slots * width * width, k, v, k, v, *late),
        name="self_back" if causal else "cross_back",
    )(q_len, k_len, q_t, k, v, g_t, lse, delta, *extra, *late)


def local(groups, tokens, enc, dec_len, enc_len, cot, sq, sqb, sk, sv, svb, so, sob, g1, s1, cq, cqb, ck, cv, cvb, co, cob,
          g2, s2, hin, hinb, hout, houtb, g3, s3, down, downb, up, upb):
    vectors = (sqb, svb, sob, g1, s1, cqb, cvb, cob, g2, s2, houtb, g3, s3, upb)
    weights = (sq, sk, sv, ck, cv, so, cq, co, down, up, hout, hin)
    remote = groups == NZ * NB
    if remote:
        arrays = [pack_vectors(vectors, hinb, downb, 1)[0], *weights]
    else:
        every = functools.partial(lax.all_gather, axis_name="tok", axis=0, tiled=True)
        packed = pack_vectors([every(v) for v in vectors], every(hinb), every(downb), NZ * NB)
        arrays = [packed.reshape(NZ, NB, 32, 128)]
        arrays += [every(w).reshape(NZ, NB, w.shape[0] * groups // (NZ * NB), w.shape[1]) for w in weights]
    arrays, kept = forward(tokens, enc, dec_len, enc_len, arrays, remote)
    flat = [a.reshape(-1, a.shape[-1]) for a in arrays[1:]]
    lse1, lse2, vec = kept[SAVED:]
    out, g3, g3b, grads, gbias = head_back(
        dec_len, kept[O_R3], cot, vec, kept[O_DB], kept[O_AB], kept[O_X2B], flat[DOWN], flat[UP]
    )
    _, bottle, width = grads.shape
    if not remote:
        parts = [grads[0].reshape(groups, -1, width), grads[1].reshape(groups, -1, width), jnp.broadcast_to(gbias[None], (groups, 8, width))]
        share = lax.psum_scatter(jnp.concatenate(parts, axis=1).astype(BF16), "tok", scatter_dimension=0, tiled=False)
    gr2, gmix, delta, shares, bias = ffn_back(
        remote, vec, g3b, kept[O_DH], flat[HOUT], flat[HIN], grads, gbias, g3, kept[O_XH2], kept[O_STAT], kept[O_CM], flat[CO]
    )
    genc, gr1, gmix, delta = attend_back(
        False, dec_len, enc_len, kept[O_CQ], kept[O_CK], kept[O_CV], gmix, lse2, delta, vec,
        (gr2, kept[O_XH1], kept[O_STAT], kept[O_SM], flat[CQ], flat[CK], flat[CV], flat[SO]),
    )
    (gtok,) = attend_back(
        True, dec_len, dec_len, kept[O_SQ], kept[O_SK], kept[O_SV], gmix, lse1, delta, vec,
        (gr1, flat[SQ], flat[SK], flat[SV]),
    )
    rows = bottle // groups
    if not remote:
        total = lax.psum(share, "grp").astype(F32)
        shares, bias = total[: 2 * rows].reshape(2, rows, width), total[2 * rows :]
    me = lax.axis_index("tok")
    up_bias = lax.dynamic_slice(bias[0], (me * (width // groups),), (width // groups,))
    down_bias = lax.dynamic_slice(bias[1], (me * rows,), (rows,))
    return out, gtok, genc, shares[0], down_bias, shares[1], up_bias


def solution(mesh):
    split = P(("grp", "tok"), None)
    two, one = P("tok", None), P("tok")
    ranks = [2, 1, 2, 2, 1, 2, 1, 1, 1, 2, 1, 2, 2, 1, 2, 1, 1, 1, 2, 1, 2, 1, 1, 1, 2, 1, 2, 1]
    return jax.shard_map(
        functools.partial(local, mesh.shape["tok"]),
        mesh=mesh,
        in_specs=(split,) * 5 + tuple(two if r == 2 else one for r in ranks),
        out_specs=(split,) * 3 + (two, one, two, one),
        check_vma=False,
    )
```
